512 devices in a mesh: dp: 32 (over z, core), tensor: 16 (over x, y).
Axes of the slice: x: 4, y: 4, z: 16, core: 2. Of those that a mesh axis runs over, the one named last changes fastest.
Arguments:
- grad_query: bfloat16 [8192, 8192], P('dp', 'tensor'), may hold values from -6 to 6
- query_weight: bfloat16 [8192, 8192], P('dp', 'tensor')
- grad_resid: bfloat16 [8192, 8192], P('dp', 'tensor'), may hold values from -6 to 6
- embeds: bfloat16 [8192, 8192], P('dp', 'tensor')
- norm_gain: float32 [8192], P('tensor'), may hold values from 0.1 to 1.9
- img_pos: int32 [32, 128], P('dp'), may hold values from 0 to 255, as said below
- img_count: int32 [32], P('dp'), may hold values from 64 to 128, as said below
- img_dest: int32 [32, 128], P('dp'), may hold values from 0 to 31, as said below
- merge_weight: bfloat16 [5120, 8192], P('dp', 'tensor'), may hold values from -0.0625 to 0.0625
- merge_pre: bfloat16 [6144, 5120], P('dp', 'tensor'), may hold values from -5 to 5
Outputs:
- grad_pre: float32 [6144, 5120], P('dp', 'tensor')
The draws below stay inside these ranges and needn't reach their ends.
Inputs may be any that keep to these rules, and one draw needn't show every extreme that they name: `img_pos`: positions of one device are distinct. `img_count`: at least 64 on every device; some device has 128. `img_dest`: among the rows of one device no encoder device is named more than 6 times; the first 6 rows of every device name one common encoder device, which so receives 6 live rows from every device.
All inputs are finite; a program needn't handle non-finite values.
Results may differ from the reference program's by a relative error of at most 0.034.
Values may be sent and summed in bfloat16 or wider, within the bound.
No kernel may reach another device: no remote copies, remote signals or barrier semaphores. Data moves between devices by JAX's collectives and lax.ppermute only.
A program may use at most 64 MiB of HBM per device.

```python
import math
import jax
import jax.numpy as jnp
from jax import lax

D = 8192
QW = 8192
MH = 5120
TOK_DEV = 256
IMG_MAX = 128
CAP = 6
ENC_DEV = 192
TOKENS = 8192
ENC_ROWS = 6144
N_DP = 32
N_TENSOR = 16


def shared_direction(key):
    return jax.random.normal(jax.random.fold_in(key, 5), (D,), jnp.float32)


def draw_query_weight(key, part):
    direction = shared_direction(key)
    key = jax.random.fold_in(key, 51)
    key_noise, key_along = jax.random.split(key)
    noise = jax.random.normal(key_noise, (D, QW), jnp.float32) * QW ** (-0.5)
    along = jax.random.normal(key_along, (QW,), jnp.float32) * QW ** (-0.5)
    return (noise + direction[:, None] * along[None, :]).astype(jnp.bfloat16)


def draw_embeds(key, part):
    direction = shared_direction(key)
    key = jax.random.fold_in(key, 11)
    key_base = jax.random.fold_in(key, 0)
    key_rows = jax.random.fold_in(key, 1)
    key_cols = jax.random.fold_in(key, 2)
    key_blocks = jax.random.fold_in(key, 4)
    key_along = jax.random.fold_in(key, 5)
    base = jax.random.normal(key_base, (TOKENS, D), jnp.float32)
    along = 1.2 * jax.random.normal(key_along, (TOKENS, 1), jnp.float32)
    base = base + along * direction[None, :]
    row_scale = jnp.exp(jax.random.uniform(key_rows, (TOKENS, 1), jnp.float32, math.log(0.3), math.log(3.0)))
    block_scale = jnp.exp(jax.random.uniform(key_blocks, (N_TENSOR,), jnp.float32, math.log(0.3), math.log(3.0)))
    col_scale = jnp.repeat(block_scale, D // N_TENSOR) * jnp.exp(jax.random.uniform(key_cols, (D,), jnp.float32, math.log(0.7), math.log(1.4)))
    return (base * row_scale * col_scale[None, :]).astype(jnp.bfloat16)


def draw_img_pos(key, part):
    key = jax.random.fold_in(key, 21)
    device_keys = jax.random.split(key, N_DP)
    return jax.vmap(lambda one_key: jax.random.permutation(one_key, TOK_DEV)[:IMG_MAX])(device_keys).astype(jnp.int32)


def draw_img_count(key, part):
    key = jax.random.fold_in(key, 31)
    key_counts, key_full = jax.random.split(key)
    counts = jax.random.randint(key_counts, (N_DP,), IMG_MAX // 2, IMG_MAX + 1)
    full_device = jax.random.randint(key_full, (), 0, N_DP)
    return jnp.where(jnp.arange(N_DP) == full_device, IMG_MAX, counts).astype(jnp.int32)


def draw_img_dest(key, part):
    key = jax.random.fold_in(key, 41)
    key_common, key_rows = jax.random.split(key)
    common_dev = jax.random.randint(key_common, (), 0, N_DP)
    slot_dev = jnp.arange(ENC_DEV, dtype=jnp.int32) // CAP

    def one_device(one_key):
        scores = jax.random.permutation(one_key, ENC_DEV).astype(jnp.int32)
        scores = jnp.where(slot_dev == common_dev, scores - ENC_DEV, scores)
        order = jnp.argsort(scores, stable=True)
        return slot_dev[order[:IMG_MAX]]
    return jax.vmap(one_device)(jax.random.split(key_rows, N_DP)).astype(jnp.int32)


def level_of(own_key, dims, shards, least, high):
    gain = 1.0
    for axis_at, blocks in shards:
        draws = jax.random.uniform(jax.random.fold_in(jax.random.fold_in(own_key, 6), axis_at), (blocks,), jnp.float32, least / len(shards), high / len(shards))
        gain = gain * jnp.repeat(jnp.exp(draws), dims[axis_at] // blocks).reshape((-1,) + (1,) * (len(dims) - 1 - axis_at))
    return gain


def gaussian(rng, shape, deviation, bound, cuts=(), kind=jnp.bfloat16):
    drawn = deviation * jax.random.normal(rng, shape, jnp.float32)
    if cuts:
        drawn = drawn * level_of(rng, shape, cuts, -0.22, 0.18)
    return jnp.clip(drawn, -bound, bound).astype(kind)


def setup_inputs(seed: int = 0) -> dict:
    key_list = jax.random.split(jax.random.key(seed), 11)
    return {
        "grad_query": gaussian(key_list[0], (TOKENS, QW), 1.0, 6.0, ((0, 32), (1, 16))),
        "query_weight": draw_query_weight(jax.random.fold_in(key_list[10], 71), 0),
        "grad_resid": gaussian(key_list[2], (TOKENS, D), 1.0, 6.0, ((0, 32), (1, 16))),
        "embeds": draw_embeds(jax.random.fold_in(key_list[10], 71), 0),
        "norm_gain": jnp.clip(1.0 + 0.18 * jax.random.normal(key_list[4], (D,), jnp.float32), 0.1, 1.9),
        "img_pos": draw_img_pos(jax.random.fold_in(key_list[10], 71), 0),
        "img_count": draw_img_count(jax.random.fold_in(key_list[10], 71), 0),
        "img_dest": draw_img_dest(jax.random.fold_in(key_list[10], 71), 0),
        "merge_weight": gaussian(key_list[8], (MH, D), D ** -0.5, 0.0625, ((0, 32), (1, 16))),
        "merge_pre": gaussian(key_list[9], (ENC_ROWS, MH), 1.0, 5.0, ((0, 32), (1, 16))),
    }


NORM_EPS = 1e-06

def gelu_slope(pre):
    value = pre.astype(jnp.float32)
    cdf_part = 0.5 * (1.0 + lax.erf(value * 0.7071067811865476))
    pdf_part = jnp.exp(-0.5 * value * value) * 0.3989422804014327
    return cdf_part + value * pdf_part

def reference(grad_query, query_weight, grad_resid, embeds, norm_gain, img_pos, img_count, img_dest, merge_weight, merge_pre):
    flat_rows = (jnp.arange(N_DP, dtype=jnp.int32)[:, None] * TOK_DEV + img_pos).reshape(-1)
    picked = jnp.take(grad_query, flat_rows, axis=0)
    query_local = QW // N_TENSOR
    normal_grad = jnp.zeros((N_DP * IMG_MAX, D), jnp.float32)
    for part_index in range(N_TENSOR):
        lower = part_index * query_local
        term = jnp.dot(picked[:, lower:lower + query_local], query_weight[:, lower:lower + query_local].T, preferred_element_type=jnp.float32)
        term = lax.optimization_barrier(term.astype(jnp.bfloat16))
        normal_grad = normal_grad + term.astype(jnp.float32)
    inputs = jnp.take(embeds, flat_rows, axis=0).astype(jnp.float32)
    residual = jnp.take(grad_resid, flat_rows, axis=0).astype(jnp.float32)
    scaled = norm_gain.astype(jnp.float32)[None, :] * normal_grad
    squares = lax.optimization_barrier(jnp.sum(inputs * inputs, axis=1))
    inner_sum = lax.optimization_barrier(jnp.sum(scaled * inputs, axis=1))
    inverse = lax.rsqrt(squares / D + NORM_EPS)
    handoff = residual + inverse[:, None] * scaled - inputs * (inverse ** 3 * inner_sum / D)[:, None]
    handoff = handoff.astype(jnp.bfloat16)
    is_live = jnp.arange(IMG_MAX, dtype=jnp.int32)[None, :] < img_count[:, None]
    dest_hot = ((img_dest[:, :, None] == jnp.arange(N_DP, dtype=jnp.int32)[None, None, :]) & is_live[:, :, None]).astype(jnp.int32)
    earlier = jnp.cumsum(dest_hot, axis=1) - dest_hot
    slot_index = lax.optimization_barrier(jnp.sum(earlier * dest_hot, axis=2))
    target = img_dest * ENC_DEV + jnp.arange(N_DP, dtype=jnp.int32)[:, None] * CAP + slot_index
    target = jnp.where(is_live, target, ENC_ROWS).astype(jnp.int32).reshape(-1)
    received = jnp.zeros((ENC_ROWS, D), jnp.bfloat16).at[target].set(handoff, mode='drop')
    model_local = D // N_TENSOR
    hidden_grad = jnp.zeros((ENC_ROWS, MH), jnp.float32)
    for part_index in range(N_TENSOR):
        lower = part_index * model_local
        term = jnp.dot(received[:, lower:lower + model_local], merge_weight[:, lower:lower + model_local].T, preferred_element_type=jnp.float32)
        term = lax.optimization_barrier(term.astype(jnp.bfloat16))
        hidden_grad = hidden_grad + term.astype(jnp.float32)
    return hidden_grad * gelu_slope(merge_pre)
```

```python
import jax
import jax.numpy as jnp
from jax import lax
from jax.experimental import pallas as pl
from jax.experimental.pallas import tpu as pltpu
from jax.sharding import PartitionSpec as P

D = 8192
NORM_EPS = 1e-06
VMEM_BYTES = 40 * 1024 * 1024


def gelu_slope(pre):
    value = pre.astype(jnp.float32)
    cdf_part = 0.5 * (1.0 + lax.erf(value * 0.7071067811865476))
    pdf_part = jnp.exp(-0.5 * value * value) * 0.3989422804014327
    return cdf_part + value * pdf_part


def product_kernel(left_ref, right_ref, out_ref):
    right = right_ref[...].reshape(-1, right_ref.shape[-1])
    out_ref[0] = lax.dot_general(
        left_ref[...], right, (((1,), (1,)), ((), ())), preferred_element_type=jnp.float32
    ).astype(out_ref.dtype)


def block_products(left, gathered, first, count, shares):
    rows, depth = left.shape
    per_share = gathered.shape[0] // shares
    return pl.pallas_call(
        product_kernel,
        grid=(shares,),
        in_specs=[
            pl.BlockSpec((rows, depth), lambda i: (0, 0)),
            pl.BlockSpec(
                (pl.Element(per_share), pl.Element(count), pl.Element(depth)),
                lambda i: (i * per_share, first, 0),
            ),
        ],
        out_specs=pl.BlockSpec((1, rows, per_share * count), lambda i: (i, 0, 0)),
        out_shape=jax.ShapeDtypeStruct((shares, rows, per_share * count), jnp.bfloat16),
        compiler_params=pltpu.CompilerParams(vmem_limit_bytes=VMEM_BYTES),
    )(left, gathered)


def local(
    grad_query,
    query_weight,
    grad_resid,
    embeds,
    norm_gain,
    img_pos,
    img_count,
    img_dest,
    merge_weight,
    merge_pre,
):
    groups = lax.axis_size("dp")
    shares = lax.axis_size("tensor")
    capacity = merge_pre.shape[0] // groups
    query_rows = query_weight.shape[0]
    merge_rows = merge_weight.shape[0]
    positions = img_pos[0]
    image_count = positions.shape[0]
    weights = lax.all_gather(jnp.concatenate([query_weight, merge_weight], axis=0), "dp", axis=0)
    picked = jnp.take(grad_query, positions, axis=0)
    inputs = jnp.take(embeds, positions, axis=0).astype(jnp.float32)
    residual = jnp.take(grad_resid, positions, axis=0).astype(jnp.float32)
    is_live = jnp.arange(image_count, dtype=jnp.int32) < img_count[0]
    target_dev = img_dest[0]
    dest_hot = (
        (target_dev[:, None] == jnp.arange(groups, dtype=jnp.int32)[None, :]) & is_live[:, None]
    ).astype(jnp.int32)
    earlier = jnp.cumsum(dest_hot, axis=0) - dest_hot
    slot_index = jnp.sum(earlier * dest_hot, axis=1)
    target = jnp.where(is_live, target_dev * capacity + slot_index, -1)
    placing = jnp.arange(groups * capacity, dtype=jnp.int32)[:, None] == target[None, :]

    partial_value = block_products(picked, weights, 0, query_rows, shares)
    normal_grad = jnp.sum(
        lax.all_to_all(partial_value, "tensor", 0, 0, tiled=True).astype(jnp.float32), axis=0
    )
    scaled = norm_gain[None, :] * normal_grad
    stats = jnp.stack([jnp.sum(inputs * inputs, axis=1), jnp.sum(scaled * inputs, axis=1)])
    stats = lax.all_to_all(
        jnp.broadcast_to(stats[None], (shares,) + stats.shape), "tensor", 0, 0, tiled=True
    )
    squares, inner_sum = jnp.sum(stats, axis=0)
    inverse = lax.rsqrt(squares / D + NORM_EPS)
    handoff = residual + inverse[:, None] * scaled - inputs * (inverse**3 * inner_sum / D)[:, None]
    handoff = handoff.astype(jnp.bfloat16)
    outbox = jnp.dot(
        placing.astype(jnp.bfloat16), handoff, preferred_element_type=jnp.float32
    ).astype(jnp.bfloat16)
    outbox = outbox.reshape(groups, capacity, handoff.shape[1])
    received = lax.all_to_all(outbox, "dp", split_axis=0, concat_axis=0, tiled=True)
    received = received.reshape(groups * capacity, handoff.shape[1])
    partial_hidden = block_products(received, weights, query_rows, merge_rows, shares)
    hidden_grad = jnp.sum(
        lax.all_to_all(partial_hidden, "tensor", 0, 0, tiled=True).astype(jnp.float32), axis=0
    )
    return hidden_grad * gelu_slope(merge_pre)


def solution(mesh):
    in_specs = (
        P("dp", "tensor"),
        P("dp", "tensor"),
        P("dp", "tensor"),
        P("dp", "tensor"),
        P("tensor"),
        P("dp", None),
        P("dp"),
        P("dp", None),
        P("dp", "tensor"),
        P("dp", "tensor"),
    )
    out_specs = P("dp", "tensor")
    return jax.shard_map(local, mesh=mesh, in_specs=in_specs, out_specs=out_specs, check_vma=False)
```

```python
import jax
import jax.numpy as jnp
from jax import lax
from jax.experimental import pallas as pl
from jax.experimental.pallas import tpu as pltpu
from jax.sharding import Mesh
from jax.sharding import PartitionSpec as P

D = 8192
NORM_EPS = 1e-06
VMEM_BYTES = 24 * 1024 * 1024
LANES = 128
DP = ("zh", "zl", "core")
TP = ("x", "y")


def gelu_slope(pre):
    value = pre.astype(jnp.float32)
    cdf_part = 0.5 * (1.0 + lax.erf(value * 0.7071067811865476))
    pdf_part = jnp.exp(-0.5 * value * value) * 0.3989422804014327
    return cdf_part + value * pdf_part


def query_kernel(rows_ref, weight_ref, out_ref, turned):
    parts, count, depth = rows_ref.shape

    @pl.when(pl.program_id(0) == 0)
    def _():
        turned[...] = rows_ref[...].reshape(parts * count, depth).T

    weight = weight_ref[...].reshape(-1, depth)
    product = jnp.dot(weight, turned[...], preferred_element_type=jnp.float32)
    product = product.astype(out_ref.dtype)
    for part in range(parts):
        out_ref[part] = product[:, part * count : (part + 1) * count]


def query_products(rows, weights):
    parts, count, depth = rows.shape
    blocks, height, _ = weights.shape
    steps = blocks // 2
    return pl.pallas_call(
        query_kernel,
        grid=(steps,),
        in_specs=[
            pl.BlockSpec((parts, count, depth), lambda i: (0, 0, 0)),
            pl.BlockSpec((2, height, depth), lambda i: (i, 0, 0)),
        ],
        out_specs=pl.BlockSpec((parts, 2 * height, count), lambda i: (i, 0, 0)),
        out_shape=jax.ShapeDtypeStruct((steps * parts, 2 * height, count), jnp.bfloat16),
        scratch_shapes=[pltpu.VMEM((depth, parts * count), jnp.bfloat16)],
        compiler_params=pltpu.CompilerParams(vmem_limit_bytes=VMEM_BYTES),
    )(rows, weights)


def handoff_kernel(capacity, grad_ref, input_ref, resid_ref, gain_ref, stat_ref, target_ref, out_ref):
    width, count = grad_ref.shape
    stats = jnp.sum(stat_ref[...], axis=0)
    inverse = lax.rsqrt(stats[0:1] / D + NORM_EPS)
    factor = inverse * inverse * inverse * stats[1:2] / D
    scaled = gain_ref[...] * grad_ref[...].astype(jnp.float32)
    handoff = (
        resid_ref[...].astype(jnp.float32)
        + inverse * scaled
        - input_ref[...].astype(jnp.float32) * factor
    ).astype(jnp.bfloat16)
    place = lax.broadcasted_iota(jnp.int32, (out_ref.shape[0], count), 0) - target_ref[...]
    total = jnp.zeros(out_ref.shape, jnp.float32)
    for block in range(width // LANES):
        hot = (place == block * capacity).astype(jnp.bfloat16)
        total += lax.dot_general(
            hot,
            handoff[block * LANES : (block + 1) * LANES],
            (((1,), (1,)), ((), ())),
            preferred_element_type=jnp.float32,
        )
    out_ref[...] = total.astype(out_ref.dtype)


def merge_kernel(capacity, box_ref, weight_ref, out_ref, turned):
    width, rows = turned.shape
    chunks = width // LANES

    @pl.when(pl.program_id(0) == 0)
    def _():
        box = box_ref[...]
        row = lax.broadcasted_iota(jnp.int32, (rows, box.shape[0]), 0)
        spot = lax.broadcasted_iota(jnp.int32, (rows, box.shape[0]), 1)
        source = (row * 10923) >> 16
        ahead = spot - (row + source * (capacity * (chunks - 1)))
        for block in range(chunks):
            hot = (ahead == block * capacity).astype(jnp.bfloat16)
            piece = jnp.dot(hot, box, preferred_element_type=jnp.float32)
            turned[block * LANES : (block + 1) * LANES] = piece.T.astype(jnp.bfloat16)

    height = weight_ref.shape[1]
    for part in range(out_ref.shape[0]):
        for half in range(2):
            product = jnp.dot(
                weight_ref[2 * part + half], turned[...], preferred_element_type=jnp.float32
            )
            out_ref[part, :, half * rows : (half + 1) * rows] = product.astype(out_ref.dtype)


def merge_products(box, weights, capacity, shares, steps):
    blocks, height, width = weights.shape
    rows = box.shape[0] * box.shape[1] // width
    per_step = shares // steps
    return pl.pallas_call(
        lambda *refs: merge_kernel(capacity, *refs),
        grid=(steps,),
        in_specs=[
            pl.BlockSpec(box.shape, lambda i: (0, 0)),
            pl.BlockSpec((blocks // steps, height, width), lambda i: (i, 0, 0)),
        ],
        out_specs=pl.BlockSpec((per_step, height, 2 * rows), lambda i: (i, 0, 0)),
        out_shape=jax.ShapeDtypeStruct((shares, height, 2 * rows), jnp.bfloat16),
        scratch_shapes=[pltpu.VMEM((width, rows), jnp.bfloat16)],
        compiler_params=pltpu.CompilerParams(vmem_limit_bytes=VMEM_BYTES),
    )(box, weights)


def local(
    grad_query,
    query_weight,
    grad_resid,
    embeds,
    norm_gain,
    img_pos,
    img_count,
    img_dest,
    merge_weight,
    merge_pre,
):
    groups = lax.axis_size(DP)
    shares = lax.axis_size(TP)
    side = lax.axis_size("zl")
    capacity = merge_pre.shape[0] // groups
    positions = img_pos[0]
    image_count = positions.shape[0]
    width = embeds.shape[1]

    query_full = lax.all_gather(query_weight, ("zh", "core"), axis=0)
    merge_weight, query_full = lax.optimization_barrier((merge_weight, query_full))
    merge_full = lax.all_gather(merge_weight, DP, axis=0)
    picked = lax.all_gather(jnp.take(grad_query, positions, axis=0), "zl", axis=0)
    inputs = jnp.take(embeds, positions, axis=0).T
    residual = jnp.take(grad_resid, positions, axis=0).T
    gain = norm_gain[:, None]
    wide = inputs.astype(jnp.float32)
    squares = jnp.sum(wide * wide, axis=0)
    is_live = jnp.arange(image_count, dtype=jnp.int32) < img_count[0]
    target_dev = img_dest[0]
    dest_hot = (
        (target_dev[:, None] == jnp.arange(groups, dtype=jnp.int32)[None, :]) & is_live[:, None]
    ).astype(jnp.int32)
    earlier = jnp.cumsum(dest_hot, axis=0) - dest_hot
    slot_index = jnp.sum(earlier * dest_hot, axis=1)
    pitch = capacity * (width // LANES)
    target = jnp.where(is_live, target_dev * pitch + slot_index, -groups * pitch)

    partial_value = query_products(picked, query_full)
    swapped = lax.all_to_all(partial_value, TP, 0, 0, tiled=True)
    normal_grad = jnp.sum(swapped.astype(jnp.float32), axis=0).astype(jnp.bfloat16)
    exchange = [(b * side + a, a * side + b) for a in range(side) for b in range(side)]
    normal_grad = lax.ppermute(normal_grad, ("zl", "y"), exchange)
    inner = jnp.sum(gain * normal_grad.astype(jnp.float32) * wide, axis=0)
    stats = jnp.stack([squares, inner])
    stats = lax.all_to_all(
        jnp.broadcast_to(stats[None], (shares,) + stats.shape), TP, 0, 0, tiled=True
    )
    outbox = pl.pallas_call(
        lambda *refs: handoff_kernel(capacity, *refs),
        out_shape=jax.ShapeDtypeStruct((groups * pitch, LANES), jnp.bfloat16),
        compiler_params=pltpu.CompilerParams(vmem_limit_bytes=VMEM_BYTES),
    )(normal_grad, inputs, residual, gain, stats, target[None])
    received = lax.all_to_all(outbox.reshape(groups, pitch, LANES), DP, 0, 0, tiled=True)
    partial_hidden = merge_products(
        received.reshape(groups * pitch, LANES), merge_full, capacity, shares, 4
    )
    hidden = lax.all_to_all(partial_hidden, TP, 0, 0, tiled=True)
    hidden = jnp.sum(hidden.astype(jnp.float32), axis=0)
    rows = merge_pre.shape[0]
    hidden = jnp.concatenate([hidden[:, :rows].T, hidden[:, rows:].T], axis=1)
    return hidden * gelu_slope(merge_pre)


def solution(mesh):
    split = Mesh(mesh.devices.reshape(4, 4, 2, 4, 4), DP + TP)
    in_specs = (
        P(DP, TP),
        P(DP, TP),
        P(DP, TP),
        P(DP, TP),
        P(TP),
        P(DP, None),
        P(DP),
        P(DP, None),
        P(DP, TP),
        P(DP, TP),
    )
    out_specs = P(DP, TP)
    return jax.shard_map(local, mesh=split, in_specs=in_specs, out_specs=out_specs, check_vma=False)
```

```python
import jax
import jax.numpy as jnp
from jax import lax
from jax.experimental import pallas as pl
from jax.experimental.pallas import tpu as pltpu
from jax.sharding import Mesh
from jax.sharding import PartitionSpec as P

D = 8192
NORM_EPS = 1e-06
MIB = 1024 * 1024
LANES = 128
SLOT_PITCH = 8
DP = ("zh", "zl", "core")
TP = ("x", "y")


def gelu_slope(pre):
    value = pre.astype(jnp.float32)
    cdf_part = 0.5 * (1.0 + lax.erf(value * 0.7071067811865476))
    pdf_part = jnp.exp(-0.5 * value * value) * 0.3989422804014327
    return cdf_part + value * pdf_part


def query_kernel(core_ref, rows_ref, own_ref, other_ref, out_ref, turned):
    parts, count, depth = rows_ref.shape
    height = own_ref.shape[1]
    core = core_ref[0]

    @pl.when(pl.program_id(0) == 0)
    def _():
        turned[...] = rows_ref[...].reshape(parts * count, depth).T

    for weight_ref, place in ((own_ref, core), (other_ref, 1 - core)):
        product = jnp.dot(weight_ref[0], turned[...], preferred_element_type=jnp.float32)
        product = product.astype(out_ref.dtype)
        spot = pl.ds(pl.multiple_of(place * height, height), height)
        for part in range(parts):
            out_ref[part, 0, spot] = product[:, part * count : (part + 1) * count]


def query_products(core, rows, own, other):
    parts, count, depth = rows.shape
    steps, height, _ = own.shape
    weight_spec = pl.BlockSpec((1, height, depth), lambda i, _: (i, 0, 0))
    return pl.pallas_call(
        query_kernel,
        grid_spec=pltpu.PrefetchScalarGridSpec(
            num_scalar_prefetch=1,
            grid=(steps,),
            in_specs=[
                pl.BlockSpec((parts, count, depth), lambda i, _: (0, 0, 0)),
                weight_spec,
                weight_spec,
            ],
            out_specs=pl.BlockSpec((parts, 1, 2 * height, count), lambda i, _: (0, i, 0, 0)),
            scratch_shapes=[pltpu.VMEM((depth, parts * count), jnp.bfloat16)],
        ),
        out_shape=jax.ShapeDtypeStruct((parts, steps, 2 * height, count), jnp.bfloat16),
        compiler_params=pltpu.CompilerParams(vmem_limit_bytes=24 * MIB),
    )(core, rows, own, other)


def merge_kernel(grad_ref, input_ref, resid_ref, gain_ref, stat_ref, weight_ref, out_ref, handoff):
    count = grad_ref.shape[1]

    @pl.when(pl.program_id(0) == 0)
    def _():
        stats = jnp.sum(stat_ref[...], axis=0)
        inverse = lax.rsqrt(stats[0:1] / D + NORM_EPS)
        factor = inverse * inverse * inverse * stats[1:2] / D
        scaled = gain_ref[...] * grad_ref[...].astype(jnp.float32)
        handoff[...] = (
            resid_ref[...].astype(jnp.float32)
            + inverse * scaled
            - input_ref[...].astype(jnp.float32) * factor
        ).astype(jnp.bfloat16)

    for part in range(out_ref.shape[0]):
        for half in range(2):
            product = jnp.dot(
                weight_ref[2 * part + half], handoff[...], preferred_element_type=jnp.float32
            )
            out_ref[part, :, half * count : (half + 1) * count] = product.astype(out_ref.dtype)


def merge_products(grad, inputs, residual, gain, stats, weights, shares, steps):
    blocks, height, width = weights.shape
    count = grad.shape[1]
    whole = [grad, inputs, residual, gain, stats]
    return pl.pallas_call(
        merge_kernel,
        grid=(steps,),
        in_specs=[
            pl.BlockSpec(a.shape, lambda i, rank=a.ndim: (0,) * rank) for a in whole
        ]
        + [pl.BlockSpec((blocks // steps, height, width), lambda i: (i, 0, 0))],
        out_specs=pl.BlockSpec((shares // steps, height, 2 * count), lambda i: (i, 0, 0)),
        out_shape=jax.ShapeDtypeStruct((shares, height, 2 * count), jnp.bfloat16),
        scratch_shapes=[pltpu.VMEM((width, count), jnp.bfloat16)],
        compiler_params=pltpu.CompilerParams(vmem_limit_bytes=56 * MIB),
    )(*whole, weights)


def send_kernel(hidden_ref, target_ref, out_ref):
    count = target_ref.shape[1]
    total = jnp.sum(hidden_ref[...].astype(jnp.float32), axis=0).astype(jnp.bfloat16)
    spare = out_ref.shape[1] - 2 * total.shape[0]
    columns = jnp.concatenate(
        [total[:, :count], total[:, count:], jnp.zeros((spare, count), jnp.bfloat16)], axis=0
    )
    row = lax.broadcasted_iota(jnp.int32, (out_ref.shape[0], count), 0)
    hot = (row == target_ref[...]).astype(jnp.bfloat16)
    out_ref[...] = lax.dot_general(
        hot, columns, (((1,), (1,)), ((), ())), preferred_element_type=jnp.float32
    ).astype(out_ref.dtype)


def finish_kernel(box_ref, spot_ref, slope_ref, out_ref):
    rows, columns = out_ref.shape
    spot = lax.broadcasted_iota(jnp.int32, (rows, box_ref.shape[0]), 1)
    hot = (spot == spot_ref[...]).astype(jnp.bfloat16)
    hidden = jnp.dot(hot, box_ref[...], preferred_element_type=jnp.float32)
    out_ref[...] = hidden[:, :columns] * slope_ref[...]


def local(
    grad_query,
    query_weight,
    grad_resid,
    embeds,
    norm_gain,
    img_pos,
    img_count,
    img_dest,
    merge_weight,
    merge_pre,
):
    groups = lax.axis_size(DP)
    shares = lax.axis_size(TP)
    side = lax.axis_size("zh")
    rows, columns = merge_pre.shape
    capacity = rows // groups
    positions = img_pos[0]
    image_count = positions.shape[0]

    own = lax.all_gather(query_weight, "zl", axis=0)
    picked = lax.all_gather(jnp.take(grad_query, positions, axis=0), "zh", axis=0)
    merge_weight, picked = lax.optimization_barrier((merge_weight, picked))
    merge_full = lax.all_gather(merge_weight, DP, axis=0)
    inputs = jnp.take(embeds, positions, axis=0).T
    residual = jnp.take(grad_resid, positions, axis=0).T
    gain = norm_gain[:, None]
    wide = inputs.astype(jnp.float32)
    squares = jnp.sum(wide * wide, axis=0)
    is_live = jnp.arange(image_count, dtype=jnp.int32) < img_count[0]
    target_dev = img_dest[0]
    dest_hot = (
        (target_dev[:, None] == jnp.arange(groups, dtype=jnp.int32)[None, :]) & is_live[:, None]
    ).astype(jnp.int32)
    earlier = jnp.cumsum(dest_hot, axis=0) - dest_hot
    slot_index = jnp.sum(earlier * dest_hot, axis=1)
    target = jnp.where(is_live, target_dev * SLOT_PITCH + slot_index, -1)
    number = jnp.arange(rows, dtype=jnp.int32)
    spot = number // capacity * SLOT_PITCH + number % capacity
    slope = gelu_slope(merge_pre)

    other = lax.ppermute(own, "core", [(0, 1), (1, 0)])
    core = lax.axis_index("core").astype(jnp.int32)[None]
    partial_value = query_products(core, picked, own, other)
    partial_value = partial_value.reshape((shares,) + partial_value.shape[2:])
    swapped = lax.all_to_all(partial_value, TP, 0, 0, tiled=True)
    normal_grad = jnp.sum(swapped.astype(jnp.float32), axis=0).astype(jnp.bfloat16)
    exchange = [(b * side + a, a * side + b) for a in range(side) for b in range(side)]
    normal_grad = lax.ppermute(normal_grad, ("zh", "x"), exchange)
    inner = jnp.sum(gain * normal_grad.astype(jnp.float32) * wide, axis=0)
    stats = jnp.stack([squares, inner])
    stats = lax.all_to_all(
        jnp.broadcast_to(stats[None], (shares,) + stats.shape), TP, 0, 0, tiled=True
    )
    partial_hidden = merge_products(
        normal_grad, inputs, residual, gain, stats, merge_full, shares, 4
    )
    hidden = lax.all_to_all(partial_hidden, TP, 0, 0, tiled=True)
    lanes = -(-columns // LANES) * LANES
    outbox = pl.pallas_call(
        send_kernel,
        out_shape=jax.ShapeDtypeStruct((groups * SLOT_PITCH, lanes), jnp.bfloat16),
        compiler_params=pltpu.CompilerParams(vmem_limit_bytes=24 * MIB),
    )(hidden, target[None])
    received = lax.all_to_all(outbox.reshape(groups, SLOT_PITCH, lanes), DP, 0, 0, tiled=True)
    return pl.pallas_call(
        finish_kernel,
        out_shape=jax.ShapeDtypeStruct((rows, columns), jnp.float32),
        compiler_params=pltpu.CompilerParams(vmem_limit_bytes=24 * MIB),
    )(received.reshape(groups * SLOT_PITCH, lanes), spot[:, None], slope)


def solution(mesh):
    split = Mesh(mesh.devices.reshape(4, 4, 2, 4, 4), DP + TP)
    in_specs = (
        P(DP, TP),
        P(DP, TP),
        P(DP, TP),
        P(DP, TP),
        P(TP),
        P(DP, None),
        P(DP),
        P(DP, None),
        P(DP, TP),
        P(DP, TP),
    )
    out_specs = P(DP, TP)
    return jax.shard_map(local, mesh=split, in_specs=in_specs, out_specs=out_specs, check_vma=False)
```

```python
import jax
import jax.numpy as jnp
from jax import lax
from jax.experimental import pallas as pl
from jax.experimental.pallas import tpu as pltpu
from jax.sharding import Mesh
from jax.sharding import PartitionSpec as P

D = 8192
NORM_EPS = 1e-06
MIB = 1024 * 1024
LANES = 128
SLOT_PITCH = 8
DP = ("zh", "zl", "core")
TP = ("x", "y")


def gelu_slope(pre):
    value = pre.astype(jnp.float32)
    cdf_part = 0.5 * (1.0 + lax.erf(value * 0.7071067811865476))
    pdf_part = jnp.exp(-0.5 * value * value) * 0.3989422804014327
    return cdf_part + value * pdf_part


def query_kernel(place_ref, rows_ref, own_ref, other_ref, out_ref, turned):
    parts, count, depth = rows_ref.shape
    height = own_ref.shape[1]
    core, shift = place_ref[0], place_ref[1]

    @pl.when(pl.program_id(0) == 0)
    def _():
        turned[...] = rows_ref[...].reshape(parts * count, depth).T

    for weight_ref, place in ((own_ref, core), (other_ref, 1 - core)):
        product = jnp.dot(weight_ref[0], turned[...], preferred_element_type=jnp.float32)
        product = product.astype(out_ref.dtype)
        spot = pl.ds(pl.multiple_of(place * height, height), height)
        for part in range(parts):
            out_ref[lax.rem(part + shift, parts), 0, spot] = product[:, part * count : (part + 1) * count]


def query_products(place, rows, own, other):
    parts, count, depth = rows.shape
    steps, height, _ = own.shape
    weight_spec = pl.BlockSpec((1, height, depth), lambda i, _: (i, 0, 0))
    return pl.pallas_call(
        query_kernel,
        grid_spec=pltpu.PrefetchScalarGridSpec(
            num_scalar_prefetch=1,
            grid=(steps,),
            in_specs=[
                pl.BlockSpec((parts, count, depth), lambda i, _: (0, 0, 0)),
                weight_spec,
                weight_spec,
            ],
            out_specs=pl.BlockSpec((parts, 1, 2 * height, count), lambda i, _: (0, i, 0, 0)),
            scratch_shapes=[pltpu.VMEM((depth, parts * count), jnp.bfloat16)],
        ),
        out_shape=jax.ShapeDtypeStruct((parts, steps, 2 * height, count), jnp.bfloat16),
        compiler_params=pltpu.CompilerParams(vmem_limit_bytes=56 * MIB),
    )(place, rows, own, other)


def merge_kernel(grad_ref, input_ref, resid_ref, gain_ref, stat_ref, weight_ref, out_ref, handoff):
    count = grad_ref.shape[1]

    @pl.when(pl.program_id(0) == 0)
    def _():
        stats = jnp.sum(stat_ref[...], axis=0)
        inverse = lax.rsqrt(stats[0:1] / D + NORM_EPS)
        factor = inverse * inverse * inverse * stats[1:2] / D
        scaled = gain_ref[...] * grad_ref[...].astype(jnp.float32)
        handoff[...] = (
            resid_ref[...].astype(jnp.float32)
            + inverse * scaled
            - input_ref[...].astype(jnp.float32) * factor
        ).astype(jnp.bfloat16)

    for part in range(out_ref.shape[0]):
        for half in range(2):
            product = jnp.dot(
                weight_ref[2 * part + half], handoff[...], preferred_element_type=jnp.float32
            )
            out_ref[part, :, half * count : (half + 1) * count] = product.astype(out_ref.dtype)


def merge_products(grad, inputs, residual, gain, stats, weights, shares, steps):
    blocks, height, width = weights.shape
    count = grad.shape[1]
    whole = [grad, inputs, residual, gain, stats]
    return pl.pallas_call(
        merge_kernel,
        grid=(steps,),
        in_specs=[
            pl.BlockSpec(a.shape, lambda i, rank=a.ndim: (0,) * rank) for a in whole
        ]
        + [pl.BlockSpec((blocks // steps, height, width), lambda i: (i, 0, 0))],
        out_specs=pl.BlockSpec((shares // steps, height, 2 * count), lambda i: (i, 0, 0)),
        out_shape=jax.ShapeDtypeStruct((shares, height, 2 * count), jnp.bfloat16),
        scratch_shapes=[pltpu.VMEM((width, count), jnp.bfloat16)],
        compiler_params=pltpu.CompilerParams(vmem_limit_bytes=56 * MIB),
    )(*whole, weights)


def send_kernel(hidden_ref, target_ref, out_ref):
    count = target_ref.shape[1]
    total = jnp.sum(hidden_ref[...].astype(jnp.float32), axis=0).astype(jnp.bfloat16)
    spare = out_ref.shape[1] - 2 * total.shape[0]
    columns = jnp.concatenate(
        [total[:, :count], total[:, count:], jnp.zeros((spare, count), jnp.bfloat16)], axis=0
    )
    row = lax.broadcasted_iota(jnp.int32, (out_ref.shape[0], count), 0)
    hot = (row == target_ref[...]).astype(jnp.bfloat16)
    out_ref[...] = lax.dot_general(
        hot, columns, (((1,), (1,)), ((), ())), preferred_element_type=jnp.float32
    ).astype(out_ref.dtype)


def finish_kernel(box_ref, spot_ref, slope_ref, out_ref):
    rows, columns = out_ref.shape
    spot = lax.broadcasted_iota(jnp.int32, (rows, box_ref.shape[0]), 1)
    hot = (spot == spot_ref[...]).astype(jnp.bfloat16)
    hidden = jnp.dot(hot, box_ref[...], preferred_element_type=jnp.float32)
    out_ref[...] = hidden[:, :columns] * slope_ref[...]


def local(
    grad_query,
    query_weight,
    grad_resid,
    embeds,
    norm_gain,
    img_pos,
    img_count,
    img_dest,
    merge_weight,
    merge_pre,
):
    groups = lax.axis_size(DP)
    shares = lax.axis_size(TP)
    side = lax.axis_size("zh")
    rows, columns = merge_pre.shape
    capacity = rows // groups
    positions = img_pos[0]
    image_count = positions.shape[0]

    own = lax.all_gather(query_weight, "zl", axis=0)
    picked = lax.all_gather(jnp.take(grad_query, positions, axis=0, mode="clip"), "zh", axis=0)
    merge_weight, picked = lax.optimization_barrier((merge_weight, picked))
    merge_full = lax.all_gather(merge_weight, DP, axis=0)
    inputs = jnp.take(embeds, positions, axis=0, mode="clip").T
    residual = jnp.take(grad_resid, positions, axis=0, mode="clip").T
    gain = norm_gain[:, None]
    wide = inputs.astype(jnp.float32)
    squares = jnp.sum(wide * wide, axis=0)
    is_live = jnp.arange(image_count, dtype=jnp.int32) < img_count[0]
    target_dev = img_dest[0]
    dest_hot = (
        (target_dev[:, None] == jnp.arange(groups, dtype=jnp.int32)[None, :]) & is_live[:, None]
    ).astype(jnp.int32)
    earlier = jnp.cumsum(dest_hot, axis=0) - dest_hot
    slot_index = jnp.sum(earlier * dest_hot, axis=1)
    target = jnp.where(is_live, target_dev * SLOT_PITCH + slot_index, -1)
    number = jnp.arange(rows, dtype=jnp.int32)
    spot = number // capacity * SLOT_PITCH + number % capacity
    slope = gelu_slope(merge_pre)

    other = lax.ppermute(own, "core", [(0, 1), (1, 0)])
    place = jnp.stack([lax.axis_index("core"), lax.axis_index("zh")]).astype(jnp.int32)
    partial_value = query_products(place, picked, own, other)
    partial_value = partial_value.reshape((shares,) + partial_value.shape[2:])
    swapped = lax.all_to_all(partial_value, TP, 0, 0, tiled=True)
    normal_grad = jnp.sum(swapped.astype(jnp.float32), axis=0).astype(jnp.bfloat16)
    exchange = [
        (h * side + (a + h) % side, a * side + h) for a in range(side) for h in range(side)
    ]
    normal_grad = lax.ppermute(normal_grad, ("zh", "x"), exchange)
    inner = jnp.sum(gain * normal_grad.astype(jnp.float32) * wide, axis=0)
    stats = jnp.stack([squares, inner])
    stats = lax.all_to_all(
        jnp.broadcast_to(stats[None], (shares,) + stats.shape), TP, 0, 0, tiled=True
    )
    partial_hidden = merge_products(
        normal_grad, inputs, residual, gain, stats, merge_full, shares, 8
    )
    hidden = lax.all_to_all(partial_hidden, TP, 0, 0, tiled=True)
    lanes = -(-columns // LANES) * LANES
    outbox = pl.pallas_call(
        send_kernel,
        out_shape=jax.ShapeDtypeStruct((groups * SLOT_PITCH, lanes), jnp.bfloat16),
        compiler_params=pltpu.CompilerParams(vmem_limit_bytes=24 * MIB),
    )(hidden, target[None])
    received = lax.all_to_all(outbox.reshape(groups, SLOT_PITCH, lanes), DP, 0, 0, tiled=True)
    return pl.pallas_call(
        finish_kernel,
        out_shape=jax.ShapeDtypeStruct((rows, columns), jnp.float32),
        compiler_params=pltpu.CompilerParams(vmem_limit_bytes=24 * MIB),
    )(received.reshape(groups * SLOT_PITCH, lanes), spot[:, None], slope)


def solution(mesh):
    split = Mesh(mesh.devices.reshape(4, 4, 2, 4, 4), DP + TP)
    in_specs = (
        P(DP, TP),
        P(DP, TP),
        P(DP, TP),
        P(DP, TP),
        P(TP),
        P(DP, None),
        P(DP),
        P(DP, None),
        P(DP, TP),
        P(DP, TP),
    )
    out_specs = P(DP, TP)
    return jax.shard_map(local, mesh=split, in_specs=in_specs, out_specs=out_specs, check_vma=False)
```

```python
import jax
import jax.numpy as jnp
from jax import lax
from jax.experimental import pallas as pl
from jax.experimental.pallas import tpu as pltpu
from jax.sharding import Mesh
from jax.sharding import PartitionSpec as P

D = 8192
NORM_EPS = 1e-06
MIB = 1024 * 1024
LANES = 128
SLOT_PITCH = 8
COPIES = 8
DP = ("zh", "zl", "core")
TP = ("x", "y")


def gelu_slope(pre):
    value = pre.astype(jnp.float32)
    cdf_part = 0.5 * (1.0 + lax.erf(value * 0.7071067811865476))
    pdf_part = jnp.exp(-0.5 * value * value) * 0.3989422804014327
    return cdf_part + value * pdf_part


def query_kernel(place_ref, rows_ref, weight_ref, *refs):
    out_ref, turned = refs[-2:]
    parts, count, depth = rows_ref.shape
    shift = place_ref[1]

    @pl.when(pl.program_id(0) == 0)
    def _():
        turned[...] = rows_ref[...].reshape(parts * count, depth).T

    product = jnp.dot(weight_ref[0], turned[...], preferred_element_type=jnp.float32)
    product = product.astype(out_ref.dtype)
    for part in range(parts):
        out_ref[lax.rem(part + shift, parts), 0, 0] = product[:, part * count : (part + 1) * count]


def query_products(place, rows, weight, flip, partly=None):
    parts, count, depth = rows.shape
    steps, height, _ = weight.shape
    out_spec = pl.BlockSpec(
        (parts, 1, 1, height, count), lambda i, place: (0, i, (place[0] + flip) % 2, 0, 0)
    )
    specs = [
        pl.BlockSpec((parts, count, depth), lambda i, _: (0, 0, 0)),
        pl.BlockSpec((1, height, depth), lambda i, _: (i, 0, 0)),
    ]
    args = [place, rows, weight]
    aliases = {}
    if partly is not None:
        specs.append(pl.BlockSpec(memory_space=pl.ANY))
        args.append(partly)
        aliases = {3: 0}
    return pl.pallas_call(
        query_kernel,
        grid_spec=pltpu.PrefetchScalarGridSpec(
            num_scalar_prefetch=1,
            grid=(steps,),
            in_specs=specs,
            out_specs=out_spec,
            scratch_shapes=[pltpu.VMEM((depth, parts * count), jnp.bfloat16)],
        ),
        out_shape=jax.ShapeDtypeStruct((parts, steps, 2, height, count), jnp.bfloat16),
        input_output_aliases=aliases,
        compiler_params=pltpu.CompilerParams(vmem_limit_bytes=16 * MIB),
    )(*args)


def reduce_kernel(place_ref, parts_ref, scaled_ref, square_ref, out_ref, stat_ref):
    total = parts_ref[0].astype(jnp.float32)
    for part in range(1, parts_ref.shape[0]):
        total += parts_ref[part].astype(jnp.float32)
    out_ref[...] = total.astype(out_ref.dtype)
    inner = jnp.sum(total * scaled_ref[...].astype(jnp.float32), axis=0, keepdims=True)
    side = stat_ref.shape[0] // 4
    for spot in range(stat_ref.shape[0]):
        plane = spot // side
        stat_ref[spot, 0:1] = jnp.where(place_ref[2] == plane, inner, 0.0)
        stat_ref[spot, 1:2] = jnp.where(place_ref[1] == plane, square_ref[...], 0.0)


def merge_kernel(
    grad_ref, input_ref, resid_ref, gain_ref, stat_ref, weight_ref, out_ref, handoff, held, sems
):
    count = grad_ref.shape[1]
    blocks, height, width = held.shape
    step = blocks // COPIES

    def copy(number):
        spot = pl.ds(number * step, step)
        return pltpu.make_async_copy(weight_ref.at[spot], held.at[spot], sems.at[number])

    for number in range(COPIES):
        copy(number).start()
    stats = jnp.sum(stat_ref[...], axis=0)
    inverse = lax.rsqrt(stats[1:2] / D + NORM_EPS)
    factor = inverse * inverse * inverse * stats[0:1] / D
    scaled = gain_ref[...] * grad_ref[...].astype(jnp.float32)
    handoff[...] = (
        resid_ref[...].astype(jnp.float32)
        + inverse * scaled
        - input_ref[...].astype(jnp.float32) * factor
    ).astype(jnp.bfloat16)
    for number in range(COPIES):
        copy(number).wait()
        weight = held[number * step : (number + 1) * step].reshape(step * height, width)
        product = jnp.dot(weight, handoff[...], preferred_element_type=jnp.float32)
        product = product.astype(out_ref.dtype)
        for block in range(step):
            share, half = divmod(number * step + block, 2)
            out_ref[share, :, half * count : (half + 1) * count] = product[
                block * height : (block + 1) * height
            ]


def merge_products(grad, inputs, residual, gain, stats, weights, shares):
    blocks, height, width = weights.shape
    count = grad.shape[1]
    local_spec = pl.BlockSpec(memory_space=pltpu.VMEM)
    return pl.pallas_call(
        merge_kernel,
        in_specs=[local_spec] * 5 + [pl.BlockSpec(memory_space=pltpu.HBM)],
        out_specs=local_spec,
        out_shape=jax.ShapeDtypeStruct((shares, height, 2 * count), jnp.bfloat16),
        scratch_shapes=[
            pltpu.VMEM((width, count), jnp.bfloat16),
            pltpu.VMEM((blocks, height, width), jnp.bfloat16),
            pltpu.SemaphoreType.DMA((COPIES,)),
        ],
        compiler_params=pltpu.CompilerParams(vmem_limit_bytes=24 * MIB),
    )(grad, inputs, residual, gain, stats, weights)


def send_kernel(hidden_ref, target_ref, out_ref):
    count = target_ref.shape[1]
    total = jnp.sum(hidden_ref[...].astype(jnp.float32), axis=0).astype(jnp.bfloat16)
    spare = out_ref.shape[1] - 2 * total.shape[0]
    columns = jnp.concatenate(
        [total[:, :count], total[:, count:], jnp.zeros((spare, count), jnp.bfloat16)], axis=0
    )
    row = lax.broadcasted_iota(jnp.int32, (out_ref.shape[0], count), 0)
    hot = (row == target_ref[...]).astype(jnp.bfloat16)
    out_ref[...] = lax.dot_general(
        hot, columns, (((1,), (1,)), ((), ())), preferred_element_type=jnp.float32
    ).astype(out_ref.dtype)


def finish_kernel(box_ref, spot_ref, slope_ref, out_ref):
    rows, columns = out_ref.shape
    spot = lax.broadcasted_iota(jnp.int32, (rows, box_ref.shape[0]), 1)
    hot = (spot == spot_ref[...]).astype(jnp.bfloat16)
    hidden = jnp.dot(hot, box_ref[...], preferred_element_type=jnp.float32)
    out_ref[...] = hidden[:, :columns] * slope_ref[...]


def local(
    grad_query,
    query_weight,
    grad_resid,
    embeds,
    norm_gain,
    img_pos,
    img_count,
    img_dest,
    merge_weight,
    merge_pre,
):
    groups = lax.axis_size(DP)
    shares = lax.axis_size(TP)
    side = lax.axis_size("zh")
    rows, columns = merge_pre.shape
    capacity = rows // groups
    positions = img_pos[0]
    image_count = positions.shape[0]
    plane = lax.axis_index("zh")
    place = jnp.stack(
        [lax.axis_index("core"), plane, (lax.axis_index("x") + side - plane) % side]
    ).astype(jnp.int32)
    forth = [(h * side + (a + h) % side, a * side + h) for a in range(side) for h in range(side)]
    back = [(target, source) for source, target in forth]

    own = lax.all_gather(query_weight, "zl", axis=0)
    picked = jnp.take(grad_query, positions, axis=0, mode="clip")
    picked = lax.all_gather(picked, "zh", axis=0)
    merge_weight, embeds, grad_resid, picked = lax.optimization_barrier(
        (merge_weight, embeds, grad_resid, picked)
    )
    merge_full = lax.all_gather(merge_weight, DP, axis=0)
    inputs = jnp.take(embeds, positions, axis=0, mode="clip").T
    residual = jnp.take(grad_resid, positions, axis=0, mode="clip").T
    gain = norm_gain[:, None]
    wide = inputs.astype(jnp.float32)
    squares = jnp.sum(wide * wide, axis=0)[None]
    scaled_input = lax.ppermute((gain * wide).astype(jnp.bfloat16), ("zh", "x"), back)
    is_live = jnp.arange(image_count, dtype=jnp.int32) < img_count[0]
    target_dev = img_dest[0]
    dest_hot = (
        (target_dev[:, None] == jnp.arange(groups, dtype=jnp.int32)[None, :]) & is_live[:, None]
    ).astype(jnp.int32)
    earlier = jnp.cumsum(dest_hot, axis=0) - dest_hot
    slot_index = jnp.sum(earlier * dest_hot, axis=1)
    target = jnp.where(is_live, target_dev * SLOT_PITCH + slot_index, -1)
    number = jnp.arange(rows, dtype=jnp.int32)
    spot = number // capacity * SLOT_PITCH + number % capacity
    slope = gelu_slope(merge_pre)

    other = lax.ppermute(own, "core", [(0, 1), (1, 0)])
    partial_value = query_products(place, picked, own, 0)
    partial_value = query_products(place, picked, other, 1, partial_value)
    width, count = inputs.shape
    swapped = lax.all_to_all(partial_value.reshape(shares, width, count), TP, 0, 0, tiled=True)
    normal_grad, stats = pl.pallas_call(
        reduce_kernel,
        in_specs=[pl.BlockSpec(memory_space=pltpu.SMEM)]
        + [pl.BlockSpec(memory_space=pltpu.VMEM)] * 3,
        out_shape=[
            jax.ShapeDtypeStruct((width, count), jnp.bfloat16),
            jax.ShapeDtypeStruct((side * side, 2, count), jnp.float32),
        ],
        compiler_params=pltpu.CompilerParams(vmem_limit_bytes=16 * MIB),
    )(place, swapped, scaled_input, squares)
    normal_grad = lax.ppermute(normal_grad, ("zh", "x"), forth)
    stats = jnp.sum(lax.all_to_all(stats, ("zh", "x"), 0, 0, tiled=True), axis=0)
    stats = lax.all_to_all(
        jnp.broadcast_to(stats[None], (side,) + stats.shape), "y", 0, 0, tiled=True
    )
    partial_hidden = merge_products(normal_grad, inputs, residual, gain, stats, merge_full, shares)
    hidden = lax.all_to_all(partial_hidden, TP, 0, 0, tiled=True)
    lanes = -(-columns // LANES) * LANES
    outbox = pl.pallas_call(
        send_kernel,
        out_shape=jax.ShapeDtypeStruct((groups * SLOT_PITCH, lanes), jnp.bfloat16),
        compiler_params=pltpu.CompilerParams(vmem_limit_bytes=16 * MIB),
    )(hidden, target[None])
    received = lax.all_to_all(outbox.reshape(groups, SLOT_PITCH, lanes), DP, 0, 0, tiled=True)
    return pl.pallas_call(
        finish_kernel,
        out_shape=jax.ShapeDtypeStruct((rows, columns), jnp.float32),
        compiler_params=pltpu.CompilerParams(vmem_limit_bytes=16 * MIB),
    )(received.reshape(groups * SLOT_PITCH, lanes), spot[:, None], slope)


def solution(mesh):
    split = Mesh(mesh.devices.reshape(4, 4, 2, 4, 4), DP + TP)
    in_specs = (
        P(DP, TP),
        P(DP, TP),
        P(DP, TP),
        P(DP, TP),
        P(TP),
        P(DP, None),
        P(DP),
        P(DP, None),
        P(DP, TP),
        P(DP, TP),
    )
    out_specs = P(DP, TP)
    return jax.shard_map(local, mesh=split, in_specs=in_specs, out_specs=out_specs, check_vma=False)
```

```python
import jax
import jax.numpy as jnp
from jax import lax
from jax.experimental import pallas as pl
from jax.experimental.pallas import tpu as pltpu
from jax.sharding import Mesh
from jax.sharding import PartitionSpec as P

D = 8192
NORM_EPS = 1e-06
MIB = 1024 * 1024
LANES = 128
DP = ("zh", "zl", "core")
TP = ("x", "y")


def gelu_slope(pre):
    value = pre.astype(jnp.float32)
    cdf_part = 0.5 * (1.0 + lax.erf(value * 0.7071067811865476))
    pdf_part = jnp.exp(-0.5 * value * value) * 0.3989422804014327
    return cdf_part + value * pdf_part


def query_kernel(core_ref, rows_ref, own_ref, other_ref, out_ref, turned):
    parts, count, depth = rows_ref.shape
    height = own_ref.shape[1]
    core = core_ref[0]

    @pl.when(pl.program_id(0) == 0)
    def _():
        turned[...] = rows_ref[...].reshape(parts * count, depth).T

    for weight_ref, place in ((own_ref, core), (other_ref, 1 - core)):
        product = jnp.dot(weight_ref[0], turned[...], preferred_element_type=jnp.float32)
        product = product.astype(out_ref.dtype)
        spot = pl.ds(pl.multiple_of(place * height, height), height)
        for part in range(parts):
            out_ref[part, spot] = product[:, part * count : (part + 1) * count]


def query_products(core, rows, own, other):
    parts, count, depth = rows.shape
    steps, height, _ = own.shape
    weight_spec = pl.BlockSpec((1, height, depth), lambda i, _: (i, 0, 0))
    return pl.pallas_call(
        query_kernel,
        grid_spec=pltpu.PrefetchScalarGridSpec(
            num_scalar_prefetch=1,
            grid=(steps,),
            in_specs=[
                pl.BlockSpec((parts, count, depth), lambda i, _: (0, 0, 0)),
                weight_spec,
                weight_spec,
            ],
            out_specs=pl.BlockSpec((parts, 2 * height, count), lambda i, _: (i, 0, 0)),
            scratch_shapes=[pltpu.VMEM((depth, parts * count), jnp.bfloat16)],
        ),
        out_shape=jax.ShapeDtypeStruct((steps * parts, 2 * height, count), jnp.bfloat16),
        compiler_params=pltpu.CompilerParams(vmem_limit_bytes=24 * MIB),
    )(core, rows, own, other)


def handoff_kernel(capacity, grad_ref, input_ref, resid_ref, gain_ref, stat_ref, target_ref, out_ref):
    width, count = grad_ref.shape
    stats = jnp.sum(stat_ref[...], axis=0)
    inverse = lax.rsqrt(stats[0:1] / D + NORM_EPS)
    factor = inverse * inverse * inverse * stats[1:2] / D
    scaled = gain_ref[...] * grad_ref[...].astype(jnp.float32)
    handoff = (
        resid_ref[...].astype(jnp.float32)
        + inverse * scaled
        - input_ref[...].astype(jnp.float32) * factor
    ).astype(jnp.bfloat16)
    place = lax.broadcasted_iota(jnp.int32, (out_ref.shape[0], count), 0) - target_ref[...]
    total = jnp.zeros(out_ref.shape, jnp.float32)
    for block in range(width // LANES):
        hot = (place == block * capacity).astype(jnp.bfloat16)
        total += lax.dot_general(
            hot,
            handoff[block * LANES : (block + 1) * LANES],
            (((1,), (1,)), ((), ())),
            preferred_element_type=jnp.float32,
        )
    out_ref[...] = total.astype(out_ref.dtype)


def merge_kernel(capacity, box_ref, weight_ref, out_ref, turned):
    width, rows = turned.shape
    chunks = width // LANES

    @pl.when(pl.program_id(0) == 0)
    def _():
        box = box_ref[...]
        row = lax.broadcasted_iota(jnp.int32, (rows, box.shape[0]), 0)
        spot = lax.broadcasted_iota(jnp.int32, (rows, box.shape[0]), 1)
        source = (row * 10923) >> 16
        ahead = spot - (row + source * (capacity * (chunks - 1)))
        for block in range(chunks):
            hot = (ahead == block * capacity).astype(jnp.bfloat16)
            piece = jnp.dot(hot, box, preferred_element_type=jnp.float32)
            turned[block * LANES : (block + 1) * LANES] = piece.T.astype(jnp.bfloat16)

    height = weight_ref.shape[1]
    for part in range(out_ref.shape[0]):
        for half in range(2):
            product = jnp.dot(
                weight_ref[2 * part + half], turned[...], preferred_element_type=jnp.float32
            )
            out_ref[part, :, half * rows : (half + 1) * rows] = product.astype(out_ref.dtype)


def merge_products(box, weights, capacity, shares, steps):
    blocks, height, width = weights.shape
    rows = box.shape[0] * box.shape[1] // width
    per_step = shares // steps
    return pl.pallas_call(
        lambda *refs: merge_kernel(capacity, *refs),
        grid=(steps,),
        in_specs=[
            pl.BlockSpec(box.shape, lambda i: (0, 0)),
            pl.BlockSpec((blocks // steps, height, width), lambda i: (i, 0, 0)),
        ],
        out_specs=pl.BlockSpec((per_step, height, 2 * rows), lambda i: (i, 0, 0)),
        out_shape=jax.ShapeDtypeStruct((shares, height, 2 * rows), jnp.bfloat16),
        scratch_shapes=[pltpu.VMEM((width, rows), jnp.bfloat16)],
        compiler_params=pltpu.CompilerParams(vmem_limit_bytes=24 * MIB),
    )(box, weights)


def local(
    grad_query,
    query_weight,
    grad_resid,
    embeds,
    norm_gain,
    img_pos,
    img_count,
    img_dest,
    merge_weight,
    merge_pre,
):
    groups = lax.axis_size(DP)
    shares = lax.axis_size(TP)
    side = lax.axis_size("zl")
    capacity = merge_pre.shape[0] // groups
    positions = img_pos[0]
    image_count = positions.shape[0]
    width = embeds.shape[1]

    own = lax.all_gather(query_weight, "zh", axis=0)
    picked = jnp.take(grad_query, positions, axis=0, mode="clip")
    picked = lax.all_gather(picked, "zl", axis=0)
    merge_weight, slope, picked = lax.optimization_barrier(
        (merge_weight, gelu_slope(merge_pre), picked)
    )
    merge_full = lax.all_gather(merge_weight, DP, axis=0)
    inputs = jnp.take(embeds, positions, axis=0, mode="clip").T
    residual = jnp.take(grad_resid, positions, axis=0, mode="clip").T
    gain = norm_gain[:, None]
    wide = inputs.astype(jnp.float32)
    squares = jnp.sum(wide * wide, axis=0)
    is_live = jnp.arange(image_count, dtype=jnp.int32) < img_count[0]
    target_dev = img_dest[0]
    dest_hot = (
        (target_dev[:, None] == jnp.arange(groups, dtype=jnp.int32)[None, :]) & is_live[:, None]
    ).astype(jnp.int32)
    earlier = jnp.cumsum(dest_hot, axis=0) - dest_hot
    slot_index = jnp.sum(earlier * dest_hot, axis=1)
    pitch = capacity * (width // LANES)
    target = jnp.where(is_live, target_dev * pitch + slot_index, -groups * pitch)

    other = lax.ppermute(own, "core", [(0, 1), (1, 0)])
    core = lax.axis_index("core").astype(jnp.int32)[None]
    partial_value = query_products(core, picked, own, other)
    swapped = lax.all_to_all(partial_value, TP, 0, 0, tiled=True)
    normal_grad = jnp.sum(swapped.astype(jnp.float32), axis=0).astype(jnp.bfloat16)
    exchange = [(b * side + a, a * side + b) for a in range(side) for b in range(side)]
    normal_grad = lax.ppermute(normal_grad, ("zl", "y"), exchange)
    inner = jnp.sum(gain * normal_grad.astype(jnp.float32) * wide, axis=0)
    stats = jnp.stack([squares, inner])
    stats = lax.all_to_all(
        jnp.broadcast_to(stats[None], (shares,) + stats.shape), TP, 0, 0, tiled=True
    )
    outbox = pl.pallas_call(
        lambda *refs: handoff_kernel(capacity, *refs),
        out_shape=jax.ShapeDtypeStruct((groups * pitch, LANES), jnp.bfloat16),
        compiler_params=pltpu.CompilerParams(vmem_limit_bytes=24 * MIB),
    )(normal_grad, inputs, residual, gain, stats, target[None])
    received = lax.all_to_all(outbox.reshape(groups, pitch, LANES), DP, 0, 0, tiled=True)
    partial_hidden = merge_products(
        received.reshape(groups * pitch, LANES), merge_full, capacity, shares, 4
    )
    hidden = lax.all_to_all(partial_hidden, TP, 0, 0, tiled=True)
    hidden = jnp.sum(hidden.astype(jnp.float32), axis=0)
    rows = merge_pre.shape[0]
    hidden = jnp.concatenate([hidden[:, :rows].T, hidden[:, rows:].T], axis=1)
    return hidden * slope


def solution(mesh):
    split = Mesh(mesh.devices.reshape(4, 4, 2, 4, 4), DP + TP)
    in_specs = (
        P(DP, TP),
        P(DP, TP),
        P(DP, TP),
        P(DP, TP),
        P(TP),
        P(DP, None),
        P(DP),
        P(DP, None),
        P(DP, TP),
        P(DP, TP),
    )
    out_specs = P(DP, TP)
    return jax.shard_map(local, mesh=split, in_specs=in_specs, out_specs=out_specs, check_vma=False)
```

```python
import jax
import jax.numpy as jnp
from jax import lax
from jax.experimental import pallas as pl
from jax.experimental.pallas import tpu as pltpu
from jax.sharding import Mesh
from jax.sharding import PartitionSpec as P

D = 8192
NORM_EPS = 1e-06
MIB = 1024 * 1024
LANES = 128
DP = ("zh", "zl", "core")
TP = ("x", "y")


def gelu_slope(pre):
    value = pre.astype(jnp.float32)
    cdf_part = 0.5 * (1.0 + lax.erf(value * 0.7071067811865476))
    pdf_part = jnp.exp(-0.5 * value * value) * 0.3989422804014327
    return cdf_part + value * pdf_part


def query_kernel(plane_ref, rows_ref, weight_ref, out_ref, turned):
    parts, count, depth = rows_ref.shape
    plane = plane_ref[0]

    @pl.when(pl.program_id(0) == 0)
    def _():
        turned[...] = rows_ref[...].reshape(parts * count, depth).T

    weight = weight_ref[...].reshape(-1, depth)
    product = jnp.dot(weight, turned[...], preferred_element_type=jnp.float32)
    product = product.astype(out_ref.dtype)
    for part in range(parts):
        out_ref[lax.rem(part + plane, parts), 0] = product[:, part * count : (part + 1) * count]


def query_products(plane, rows, weights):
    parts, count, depth = rows.shape
    blocks, height, _ = weights.shape
    steps = blocks // 2
    result = pl.pallas_call(
        query_kernel,
        grid_spec=pltpu.PrefetchScalarGridSpec(
            num_scalar_prefetch=1,
            grid=(steps,),
            in_specs=[
                pl.BlockSpec((parts, count, depth), lambda i, _: (0, 0, 0)),
                pl.BlockSpec((2, height, depth), lambda i, _: (i, 0, 0)),
            ],
            out_specs=pl.BlockSpec((parts, 1, 2 * height, count), lambda i, _: (0, i, 0, 0)),
            scratch_shapes=[pltpu.VMEM((depth, parts * count), jnp.bfloat16)],
        ),
        out_shape=jax.ShapeDtypeStruct((parts, steps, 2 * height, count), jnp.bfloat16),
        compiler_params=pltpu.CompilerParams(vmem_limit_bytes=16 * MIB),
    )(plane, rows, weights)
    return result.reshape(parts * steps, 2 * height, count)


def handoff_kernel(
    capacity, early_ref, late_ref, input_ref, resid_ref, gain_ref, stat_ref, target_ref, out_ref
):
    width, count = input_ref.shape
    fourth = width // 4
    grad = jnp.concatenate(
        [
            early_ref[:fourth].astype(jnp.float32),
            late_ref[:fourth].astype(jnp.float32),
            early_ref[fourth:].astype(jnp.float32),
            late_ref[fourth:].astype(jnp.float32),
        ],
        axis=0,
    )
    stats = jnp.sum(stat_ref[...], axis=0)
    inverse = lax.rsqrt(stats[0:1] / D + NORM_EPS)
    factor = inverse * inverse * inverse * stats[1:2] / D
    scaled = gain_ref[...] * grad
    handoff = (
        resid_ref[...].astype(jnp.float32)
        + inverse * scaled
        - input_ref[...].astype(jnp.float32) * factor
    ).astype(jnp.bfloat16)
    place = lax.broadcasted_iota(jnp.int32, (out_ref.shape[0], count), 0) - target_ref[...]
    total = jnp.zeros(out_ref.shape, jnp.float32)
    for block in range(width // LANES):
        hot = (place == block * capacity).astype(jnp.bfloat16)
        total += lax.dot_general(
            hot,
            handoff[block * LANES : (block + 1) * LANES],
            (((1,), (1,)), ((), ())),
            preferred_element_type=jnp.float32,
        )
    out_ref[...] = total.astype(out_ref.dtype)


def merge_kernel(capacity, box_ref, weight_ref, out_ref, turned):
    width, rows = turned.shape
    chunks = width // LANES

    @pl.when(pl.program_id(0) == 0)
    def _():
        box = box_ref[...]
        row = lax.broadcasted_iota(jnp.int32, (rows, box.shape[0]), 0)
        spot = lax.broadcasted_iota(jnp.int32, (rows, box.shape[0]), 1)
        source = (row * 10923) >> 16
        ahead = spot - (row + source * (capacity * (chunks - 1)))
        for block in range(chunks):
            hot = (ahead == block * capacity).astype(jnp.bfloat16)
            piece = jnp.dot(hot, box, preferred_element_type=jnp.float32)
            turned[block * LANES : (block + 1) * LANES] = piece.T.astype(jnp.bfloat16)

    height = weight_ref.shape[1]
    for part in range(out_ref.shape[0]):
        for half in range(2):
            product = jnp.dot(
                weight_ref[2 * part + half], turned[...], preferred_element_type=jnp.float32
            )
            out_ref[part, :, half * rows : (half + 1) * rows] = product.astype(out_ref.dtype)


def merge_products(box, weights, capacity, shares, steps):
    blocks, height, width = weights.shape
    rows = box.shape[0] * box.shape[1] // width
    per_step = shares // steps
    return pl.pallas_call(
        lambda *refs: merge_kernel(capacity, *refs),
        grid=(steps,),
        in_specs=[
            pl.BlockSpec(box.shape, lambda i: (0, 0)),
            pl.BlockSpec((blocks // steps, height, width), lambda i: (i, 0, 0)),
        ],
        out_specs=pl.BlockSpec((per_step, height, 2 * rows), lambda i: (i, 0, 0)),
        out_shape=jax.ShapeDtypeStruct((shares, height, 2 * rows), jnp.bfloat16),
        scratch_shapes=[pltpu.VMEM((width, rows), jnp.bfloat16)],
        compiler_params=pltpu.CompilerParams(vmem_limit_bytes=24 * MIB),
    )(box, weights)


def local(
    grad_query,
    query_weight,
    grad_resid,
    embeds,
    norm_gain,
    img_pos,
    img_count,
    img_dest,
    merge_weight,
    merge_pre,
):
    groups = lax.axis_size(DP)
    shares = lax.axis_size(TP)
    side = lax.axis_size("zh")
    capacity = merge_pre.shape[0] // groups
    positions = img_pos[0]
    image_count = positions.shape[0]
    width = embeds.shape[1]

    half = query_weight.shape[0] // 2
    weights = [
        lax.all_gather(query_weight[:half], ("zl", "core"), axis=0),
        lax.all_gather(query_weight[half:], ("zl", "core"), axis=0),
    ]
    picked = jnp.take(grad_query, positions, axis=0, mode="clip")
    picked = lax.all_gather(picked, "zh", axis=0)
    merge_weight, slope, picked, weights[0] = lax.optimization_barrier(
        (merge_weight, gelu_slope(merge_pre), picked, weights[0])
    )
    merge_full = lax.all_gather(merge_weight, DP, axis=0)
    inputs = jnp.take(embeds, positions, axis=0, mode="clip").T
    residual = jnp.take(grad_resid, positions, axis=0, mode="clip").T
    gain = norm_gain[:, None]
    wide = inputs.astype(jnp.float32)
    squares = jnp.sum(wide * wide, axis=0)
    is_live = jnp.arange(image_count, dtype=jnp.int32) < img_count[0]
    target_dev = img_dest[0]
    dest_hot = (
        (target_dev[:, None] == jnp.arange(groups, dtype=jnp.int32)[None, :]) & is_live[:, None]
    ).astype(jnp.int32)
    earlier = jnp.cumsum(dest_hot, axis=0) - dest_hot
    slot_index = jnp.sum(earlier * dest_hot, axis=1)
    pitch = capacity * (width // LANES)
    target = jnp.where(is_live, target_dev * pitch + slot_index, -groups * pitch)

    plane = lax.axis_index("zh").astype(jnp.int32)[None]
    forth = [(h * side + (a + h) % side, a * side + h) for a in range(side) for h in range(side)]
    scaled_input = (gain * wide).reshape(2, 2, half, image_count)
    grads, inner = [], 0.0
    for part in range(2):
        sums = lax.all_to_all(query_products(plane, picked, weights[part]), TP, 0, 0, tiled=True)
        grad = jnp.sum(sums.astype(jnp.float32), axis=0).astype(jnp.bfloat16)
        grad = lax.ppermute(grad, ("zh", "x"), forth)
        piece = grad.astype(jnp.float32).reshape(2, half, image_count)
        inner += jnp.sum(piece * scaled_input[:, part], axis=(0, 1))
        grads.append(grad)
    stats = jnp.stack([squares, inner])
    stats = lax.all_to_all(
        jnp.broadcast_to(stats[None], (shares,) + stats.shape), TP, 0, 0, tiled=True
    )
    outbox = pl.pallas_call(
        lambda *refs: handoff_kernel(capacity, *refs),
        out_shape=jax.ShapeDtypeStruct((groups * pitch, LANES), jnp.bfloat16),
        compiler_params=pltpu.CompilerParams(vmem_limit_bytes=24 * MIB),
    )(*grads, inputs, residual, gain, stats, target[None])
    received = lax.all_to_all(outbox.reshape(groups, pitch, LANES), DP, 0, 0, tiled=True)
    partial_hidden = merge_products(
        received.reshape(groups * pitch, LANES), merge_full, capacity, shares, 4
    )
    hidden = lax.all_to_all(partial_hidden, TP, 0, 0, tiled=True)
    hidden = jnp.sum(hidden.astype(jnp.float32), axis=0)
    rows = merge_pre.shape[0]
    hidden = jnp.concatenate([hidden[:, :rows].T, hidden[:, rows:].T], axis=1)
    return hidden * slope


def solution(mesh):
    split = Mesh(mesh.devices.reshape(4, 4, 2, 4, 4), DP + TP)
    in_specs = (
        P(DP, TP),
        P(DP, TP),
        P(DP, TP),
        P(DP, TP),
        P(TP),
        P(DP, None),
        P(DP),
        P(DP, None),
        P(DP, TP),
        P(DP, TP),
    )
    out_specs = P(DP, TP)
    return jax.shard_map(local, mesh=split, in_specs=in_specs, out_specs=out_specs, check_vma=False)
```

```python
import jax
import jax.numpy as jnp
from jax import lax
from jax.experimental import pallas as pl
from jax.experimental.pallas import tpu as pltpu
from jax.sharding import Mesh
from jax.sharding import PartitionSpec as P

D = 8192
NORM_EPS = 1e-06
MIB = 1024 * 1024
LANES = 128
SLOT_PITCH = 8
DP = ("zh", "zl", "core")
TP = ("x", "y")


def gelu_slope(pre):
    value = pre.astype(jnp.float32)
    cdf_part = 0.5 * (1.0 + lax.erf(value * 0.7071067811865476))
    pdf_part = jnp.exp(-0.5 * value * value) * 0.3989422804014327
    return cdf_part + value * pdf_part


def query_kernel(place_ref, rows_ref, own_ref, other_ref, out_ref, turned):
    parts, count, depth = rows_ref.shape
    height = own_ref.shape[1]
    core, shift = place_ref[0], place_ref[1]

    @pl.when(pl.program_id(0) == 0)
    def _():
        turned[...] = rows_ref[...].reshape(parts * count, depth).T

    for weight_ref, place in ((own_ref, core), (other_ref, 1 - core)):
        product = jnp.dot(weight_ref[0], turned[...], preferred_element_type=jnp.float32)
        product = product.astype(out_ref.dtype)
        spot = pl.ds(pl.multiple_of(place * height, height), height)
        for part in range(parts):
            out_ref[lax.rem(part + shift, parts), 0, spot] = product[:, part * count : (part + 1) * count]


def query_products(place, rows, own, other):
    parts, count, depth = rows.shape
    steps, height, _ = own.shape
    weight_spec = pl.BlockSpec((1, height, depth), lambda i, _: (i, 0, 0))
    return pl.pallas_call(
        query_kernel,
        grid_spec=pltpu.PrefetchScalarGridSpec(
            num_scalar_prefetch=1,
            grid=(steps,),
            in_specs=[
                pl.BlockSpec((parts, count, depth), lambda i, _: (0, 0, 0)),
                weight_spec,
                weight_spec,
            ],
            out_specs=pl.BlockSpec((parts, 1, 2 * height, count), lambda i, _: (0, i, 0, 0)),
            scratch_shapes=[pltpu.VMEM((depth, parts * count), jnp.bfloat16)],
        ),
        out_shape=jax.ShapeDtypeStruct((parts, steps, 2 * height, count), jnp.bfloat16),
        compiler_params=pltpu.CompilerParams(vmem_limit_bytes=24 * MIB),
    )(place, rows, own, other)


def merge_kernel(grad_ref, input_ref, resid_ref, gain_ref, stat_ref, weight_ref, out_ref, handoff):
    count = grad_ref.shape[1]

    @pl.when(pl.program_id(0) == 0)
    def _():
        stats = jnp.sum(stat_ref[...], axis=0)
        inverse = lax.rsqrt(stats[0:1] / D + NORM_EPS)
        factor = inverse * inverse * inverse * stats[1:2] / D
        scaled = gain_ref[...] * grad_ref[...].astype(jnp.float32)
        handoff[...] = (
            resid_ref[...].astype(jnp.float32)
            + inverse * scaled
            - input_ref[...].astype(jnp.float32) * factor
        ).astype(jnp.bfloat16)

    for part in range(out_ref.shape[0]):
        for half in range(2):
            product = jnp.dot(
                weight_ref[2 * part + half], handoff[...], preferred_element_type=jnp.float32
            )
            out_ref[part, :, half * count : (half + 1) * count] = product.astype(out_ref.dtype)


def merge_products(grad, inputs, residual, gain, stats, weights, shares, steps):
    blocks, height, width = weights.shape
    count = grad.shape[1]
    whole = [grad, inputs, residual, gain, stats]
    return pl.pallas_call(
        merge_kernel,
        grid=(steps,),
        in_specs=[
            pl.BlockSpec(a.shape, lambda i, rank=a.ndim: (0,) * rank) for a in whole
        ]
        + [pl.BlockSpec((blocks // steps, height, width), lambda i: (i, 0, 0))],
        out_specs=pl.BlockSpec((shares // steps, height, 2 * count), lambda i: (i, 0, 0)),
        out_shape=jax.ShapeDtypeStruct((shares, height, 2 * count), jnp.bfloat16),
        scratch_shapes=[pltpu.VMEM((width, count), jnp.bfloat16)],
        compiler_params=pltpu.CompilerParams(vmem_limit_bytes=24 * MIB),
    )(*whole, weights)


def send_kernel(hidden_ref, target_ref, out_ref):
    count = target_ref.shape[1]
    total = jnp.sum(hidden_ref[...].astype(jnp.float32), axis=0).astype(jnp.bfloat16)
    spare = out_ref.shape[1] - 2 * total.shape[0]
    columns = jnp.concatenate(
        [total[:, :count], total[:, count:], jnp.zeros((spare, count), jnp.bfloat16)], axis=0
    )
    row = lax.broadcasted_iota(jnp.int32, (out_ref.shape[0], count), 0)
    hot = (row == target_ref[...]).astype(jnp.bfloat16)
    out_ref[...] = lax.dot_general(
        hot, columns, (((1,), (1,)), ((), ())), preferred_element_type=jnp.float32
    ).astype(out_ref.dtype)


def finish_kernel(box_ref, spot_ref, slope_ref, out_ref):
    rows, columns = out_ref.shape
    spot = lax.broadcasted_iota(jnp.int32, (rows, box_ref.shape[0]), 1)
    hot = (spot == spot_ref[...]).astype(jnp.bfloat16)
    hidden = jnp.dot(hot, box_ref[...], preferred_element_type=jnp.float32)
    out_ref[...] = hidden[:, :columns] * slope_ref[...]


def local(
    grad_query,
    query_weight,
    grad_resid,
    embeds,
    norm_gain,
    img_pos,
    img_count,
    img_dest,
    merge_weight,
    merge_pre,
):
    groups = lax.axis_size(DP)
    shares = lax.axis_size(TP)
    side = lax.axis_size("zh")
    rows, columns = merge_pre.shape
    capacity = rows // groups
    positions = img_pos[0]
    image_count = positions.shape[0]

    own = lax.all_gather(query_weight, "zl", axis=0)
    picked = lax.all_gather(jnp.take(grad_query, positions, axis=0, mode="clip"), "zh", axis=0)
    merge_weight, picked = lax.optimization_barrier((merge_weight, picked))
    merge_full = lax.all_gather(merge_weight, DP, axis=0)
    inputs = jnp.take(embeds, positions, axis=0, mode="clip").T
    residual = jnp.take(grad_resid, positions, axis=0, mode="clip").T
    gain = norm_gain[:, None]
    wide = inputs.astype(jnp.float32)
    squares = jnp.sum(wide * wide, axis=0)
    is_live = jnp.arange(image_count, dtype=jnp.int32) < img_count[0]
    target_dev = img_dest[0]
    dest_hot = (
        (target_dev[:, None] == jnp.arange(groups, dtype=jnp.int32)[None, :]) & is_live[:, None]
    ).astype(jnp.int32)
    earlier = jnp.cumsum(dest_hot, axis=0) - dest_hot
    slot_index = jnp.sum(earlier * dest_hot, axis=1)
    target = jnp.where(is_live, target_dev * SLOT_PITCH + slot_index, -1)
    number = jnp.arange(rows, dtype=jnp.int32)
    spot = number // capacity * SLOT_PITCH + number % capacity
    slope = gelu_slope(merge_pre)

    other = lax.ppermute(own, "core", [(0, 1), (1, 0)])
    place = jnp.stack([lax.axis_index("core"), lax.axis_index("zh")]).astype(jnp.int32)
    partial_value = query_products(place, picked, own, other)
    partial_value = partial_value.reshape((shares,) + partial_value.shape[2:])
    swapped = lax.all_to_all(partial_value, TP, 0, 0, tiled=True)
    normal_grad = jnp.sum(swapped.astype(jnp.float32), axis=0).astype(jnp.bfloat16)
    exchange = [
        (h * side + (a + h) % side, a * side + h) for a in range(side) for h in range(side)
    ]
    normal_grad = lax.ppermute(normal_grad, ("zh", "x"), exchange)
    inner = jnp.sum(gain * normal_grad.astype(jnp.float32) * wide, axis=0)
    stats = jnp.stack([squares, inner])
    stats = lax.all_to_all(
        jnp.broadcast_to(stats[None], (shares,) + stats.shape), TP, 0, 0, tiled=True
    )
    partial_hidden = merge_products(
        normal_grad, inputs, residual, gain, stats, merge_full, shares, 4
    )
    hidden = lax.all_to_all(partial_hidden, TP, 0, 0, tiled=True)
    lanes = -(-columns // LANES) * LANES
    outbox = pl.pallas_call(
        send_kernel,
        out_shape=jax.ShapeDtypeStruct((groups * SLOT_PITCH, lanes), jnp.bfloat16),
        compiler_params=pltpu.CompilerParams(vmem_limit_bytes=24 * MIB),
    )(hidden, target[None])
    received = lax.all_to_all(outbox.reshape(groups, SLOT_PITCH, lanes), DP, 0, 0, tiled=True)
    return pl.pallas_call(
        finish_kernel,
        out_shape=jax.ShapeDtypeStruct((rows, columns), jnp.float32),
        compiler_params=pltpu.CompilerParams(vmem_limit_bytes=24 * MIB),
    )(received.reshape(groups * SLOT_PITCH, lanes), spot[:, None], slope)


def solution(mesh):
    split = Mesh(mesh.devices.reshape(4, 4, 2, 4, 4), DP + TP)
    in_specs = (
        P(DP, TP),
        P(DP, TP),
        P(DP, TP),
        P(DP, TP),
        P(TP),
        P(DP, None),
        P(DP),
        P(DP, None),
        P(DP, TP),
        P(DP, TP),
    )
    out_specs = P(DP, TP)
    return jax.shard_map(local, mesh=split, in_specs=in_specs, out_specs=out_specs, check_vma=False)
```

```python
import jax
import jax.numpy as jnp
from jax import lax
from jax.experimental import pallas as pl
from jax.experimental.pallas import tpu as pltpu
from jax.sharding import Mesh
from jax.sharding import PartitionSpec as P

D = 8192
NORM_EPS = 1e-06
MIB = 1024 * 1024
LANES = 128
SLOT_PITCH = 8
COPIES = 8
DP = ("zh", "zl", "core")
TP = ("x", "y")


def gelu_slope(pre):
    value = pre.astype(jnp.float32)
    cdf_part = 0.5 * (1.0 + lax.erf(value * 0.7071067811865476))
    pdf_part = jnp.exp(-0.5 * value * value) * 0.3989422804014327
    return cdf_part + value * pdf_part


def query_kernel(place_ref, rows_ref, own_ref, other_ref, out_ref, turned):
    parts, count, depth = rows_ref.shape
    height = own_ref.shape[1]
    core, shift = place_ref[0], place_ref[1]

    @pl.when(pl.program_id(0) == 0)
    def _():
        turned[...] = rows_ref[...].reshape(parts * count, depth).T

    for weight_ref, place in ((own_ref, core), (other_ref, 1 - core)):
        product = jnp.dot(weight_ref[0], turned[...], preferred_element_type=jnp.float32)
        product = product.astype(out_ref.dtype)
        spot = pl.ds(pl.multiple_of(place * height, height), height)
        for part in range(parts):
            out_ref[lax.rem(part + shift, parts), 0, spot] = product[:, part * count : (part + 1) * count]


def query_products(place, rows, own, other):
    parts, count, depth = rows.shape
    steps, height, _ = own.shape
    weight_spec = pl.BlockSpec((1, height, depth), lambda i, _: (i, 0, 0))
    return pl.pallas_call(
        query_kernel,
        grid_spec=pltpu.PrefetchScalarGridSpec(
            num_scalar_prefetch=1,
            grid=(steps,),
            in_specs=[
                pl.BlockSpec((parts, count, depth), lambda i, _: (0, 0, 0)),
                weight_spec,
                weight_spec,
            ],
            out_specs=pl.BlockSpec((parts, 1, 2 * height, count), lambda i, _: (0, i, 0, 0)),
            scratch_shapes=[pltpu.VMEM((depth, parts * count), jnp.bfloat16)],
        ),
        out_shape=jax.ShapeDtypeStruct((parts, steps, 2 * height, count), jnp.bfloat16),
        compiler_params=pltpu.CompilerParams(vmem_limit_bytes=24 * MIB),
    )(place, rows, own, other)


def merge_kernel(
    grad_ref, input_ref, resid_ref, gain_ref, stat_ref, weight_ref, out_ref, handoff, held, sems
):
    count = grad_ref.shape[1]
    blocks, height, width = held.shape
    step = blocks // COPIES

    def copy(number):
        spot = pl.ds(number * step, step)
        return pltpu.make_async_copy(weight_ref.at[spot], held.at[spot], sems.at[number])

    for number in range(COPIES):
        copy(number).start()
    stats = jnp.sum(stat_ref[...], axis=0)
    inverse = lax.rsqrt(stats[0:1] / D + NORM_EPS)
    factor = inverse * inverse * inverse * stats[1:2] / D
    scaled = gain_ref[...] * grad_ref[...].astype(jnp.float32)
    handoff[...] = (
        resid_ref[...].astype(jnp.float32)
        + inverse * scaled
        - input_ref[...].astype(jnp.float32) * factor
    ).astype(jnp.bfloat16)
    for number in range(COPIES):
        copy(number).wait()
        weight = held[number * step : (number + 1) * step].reshape(step * height, width)
        product = jnp.dot(weight, handoff[...], preferred_element_type=jnp.float32)
        product = product.astype(out_ref.dtype)
        for block in range(step):
            share, half = divmod(number * step + block, 2)
            out_ref[share, :, half * count : (half + 1) * count] = product[
                block * height : (block + 1) * height
            ]


def merge_products(grad, inputs, residual, gain, stats, weights, shares):
    blocks, height, width = weights.shape
    count = grad.shape[1]
    local_spec = pl.BlockSpec(memory_space=pltpu.VMEM)
    return pl.pallas_call(
        merge_kernel,
        in_specs=[local_spec] * 5 + [pl.BlockSpec(memory_space=pl.ANY)],
        out_specs=local_spec,
        out_shape=jax.ShapeDtypeStruct((shares, height, 2 * count), jnp.bfloat16),
        scratch_shapes=[
            pltpu.VMEM((width, count), jnp.bfloat16),
            pltpu.VMEM((blocks, height, width), jnp.bfloat16),
            pltpu.SemaphoreType.DMA((COPIES,)),
        ],
        compiler_params=pltpu.CompilerParams(vmem_limit_bytes=56 * MIB),
    )(grad, inputs, residual, gain, stats, weights)


def send_kernel(hidden_ref, target_ref, out_ref):
    count = target_ref.shape[1]
    total = jnp.sum(hidden_ref[...].astype(jnp.float32), axis=0).astype(jnp.bfloat16)
    spare = out_ref.shape[1] - 2 * total.shape[0]
    columns = jnp.concatenate(
        [total[:, :count], total[:, count:], jnp.zeros((spare, count), jnp.bfloat16)], axis=0
    )
    row = lax.broadcasted_iota(jnp.int32, (out_ref.shape[0], count), 0)
    hot = (row == target_ref[...]).astype(jnp.bfloat16)
    out_ref[...] = lax.dot_general(
        hot, columns, (((1,), (1,)), ((), ())), preferred_element_type=jnp.float32
    ).astype(out_ref.dtype)


def finish_kernel(box_ref, spot_ref, slope_ref, out_ref):
    rows, columns = out_ref.shape
    spot = lax.broadcasted_iota(jnp.int32, (rows, box_ref.shape[0]), 1)
    hot = (spot == spot_ref[...]).astype(jnp.bfloat16)
    hidden = jnp.dot(hot, box_ref[...], preferred_element_type=jnp.float32)
    out_ref[...] = hidden[:, :columns] * slope_ref[...]


def local(
    grad_query,
    query_weight,
    grad_resid,
    embeds,
    norm_gain,
    img_pos,
    img_count,
    img_dest,
    merge_weight,
    merge_pre,
):
    groups = lax.axis_size(DP)
    shares = lax.axis_size(TP)
    side = lax.axis_size("zh")
    rows, columns = merge_pre.shape
    capacity = rows // groups
    positions = img_pos[0]
    image_count = positions.shape[0]

    own = lax.all_gather(query_weight, "zl", axis=0)
    picked = jnp.take(grad_query, positions, axis=0, mode="clip")
    inputs = jnp.take(embeds, positions, axis=0, mode="clip").T
    residual = jnp.take(grad_resid, positions, axis=0, mode="clip").T
    gain = norm_gain[:, None]
    wide = inputs.astype(jnp.float32)
    squares = jnp.sum(wide * wide, axis=0)
    is_live = jnp.arange(image_count, dtype=jnp.int32) < img_count[0]
    target_dev = img_dest[0]
    dest_hot = (
        (target_dev[:, None] == jnp.arange(groups, dtype=jnp.int32)[None, :]) & is_live[:, None]
    ).astype(jnp.int32)
    earlier = jnp.cumsum(dest_hot, axis=0) - dest_hot
    slot_index = jnp.sum(earlier * dest_hot, axis=1)
    target = jnp.where(is_live, target_dev * SLOT_PITCH + slot_index, -1)
    number = jnp.arange(rows, dtype=jnp.int32)
    spot = number // capacity * SLOT_PITCH + number % capacity
    slope = gelu_slope(merge_pre)
    picked, inputs, residual, squares, target, slope = lax.optimization_barrier(
        (picked, inputs, residual, squares, target, slope)
    )
    wide = inputs.astype(jnp.float32)
    picked = lax.all_gather(picked, "zh", axis=0)
    merge_weight, picked = lax.optimization_barrier((merge_weight, picked))
    merge_full = lax.all_gather(merge_weight, DP, axis=0)

    other = lax.ppermute(own, "core", [(0, 1), (1, 0)])
    place = jnp.stack([lax.axis_index("core"), lax.axis_index("zh")]).astype(jnp.int32)
    partial_value = query_products(place, picked, own, other)
    partial_value = partial_value.reshape((shares,) + partial_value.shape[2:])
    swapped = lax.all_to_all(partial_value, TP, 0, 0, tiled=True)
    normal_grad = jnp.sum(swapped.astype(jnp.float32), axis=0).astype(jnp.bfloat16)
    exchange = [
        (h * side + (a + h) % side, a * side + h) for a in range(side) for h in range(side)
    ]
    normal_grad = lax.ppermute(normal_grad, ("zh", "x"), exchange)
    inner = jnp.sum(gain * normal_grad.astype(jnp.float32) * wide, axis=0)
    stats = jnp.stack([squares, inner])
    stats = lax.all_to_all(
        jnp.broadcast_to(stats[None], (shares,) + stats.shape), TP, 0, 0, tiled=True
    )
    partial_hidden = merge_products(normal_grad, inputs, residual, gain, stats, merge_full, shares)
    hidden = lax.all_to_all(partial_hidden, TP, 0, 0, tiled=True)
    lanes = -(-columns // LANES) * LANES
    outbox = pl.pallas_call(
        send_kernel,
        out_shape=jax.ShapeDtypeStruct((groups * SLOT_PITCH, lanes), jnp.bfloat16),
        compiler_params=pltpu.CompilerParams(vmem_limit_bytes=24 * MIB),
    )(hidden, target[None])
    received = lax.all_to_all(outbox.reshape(groups, SLOT_PITCH, lanes), DP, 0, 0, tiled=True)
    return pl.pallas_call(
        finish_kernel,
        out_shape=jax.ShapeDtypeStruct((rows, columns), jnp.float32),
        compiler_params=pltpu.CompilerParams(vmem_limit_bytes=24 * MIB),
    )(received.reshape(groups * SLOT_PITCH, lanes), spot[:, None], slope)


def solution(mesh):
    split = Mesh(mesh.devices.reshape(4, 4, 2, 4, 4), DP + TP)
    in_specs = (
        P(DP, TP),
        P(DP, TP),
        P(DP, TP),
        P(DP, TP),
        P(TP),
        P(DP, None),
        P(DP),
        P(DP, None),
        P(DP, TP),
        P(DP, TP),
    )
    out_specs = P(DP, TP)
    return jax.shard_map(local, mesh=split, in_specs=in_specs, out_specs=out_specs, check_vma=False)
```

```python
import jax
import jax.numpy as jnp
from jax import lax
from jax.experimental import pallas as pl
from jax.experimental.pallas import tpu as pltpu
from jax.sharding import Mesh
from jax.sharding import PartitionSpec as P

D = 8192
NORM_EPS = 1e-06
MIB = 1024 * 1024
LANES = 128
SLOT_PITCH = 8
DP = ("zh", "zl", "core")
TP = ("x", "y")


def gelu_slope(pre):
    value = pre.astype(jnp.float32)
    cdf_part = 0.5 * (1.0 + lax.erf(value * 0.7071067811865476))
    pdf_part = jnp.exp(-0.5 * value * value) * 0.3989422804014327
    return cdf_part + value * pdf_part


def query_kernel(place_ref, rows_ref, own_ref, other_ref, out_ref, turned):
    parts, count, depth = rows_ref.shape
    height = own_ref.shape[1]
    core, shift = place_ref[0], place_ref[1]

    @pl.when(pl.program_id(0) == 0)
    def _():
        turned[...] = rows_ref[...].reshape(parts * count, depth).T

    for weight_ref, place in ((own_ref, core), (other_ref, 1 - core)):
        product = jnp.dot(weight_ref[0], turned[...], preferred_element_type=jnp.float32)
        product = product.astype(out_ref.dtype)
        spot = pl.ds(pl.multiple_of(place * height, height), height)
        for part in range(parts):
            out_ref[lax.rem(part + shift, parts), 0, spot] = product[:, part * count : (part + 1) * count]


def query_products(place, rows, own, other):
    parts, count, depth = rows.shape
    steps, height, _ = own.shape
    weight_spec = pl.BlockSpec((1, height, depth), lambda i, _: (i, 0, 0))
    return pl.pallas_call(
        query_kernel,
        grid_spec=pltpu.PrefetchScalarGridSpec(
            num_scalar_prefetch=1,
            grid=(steps,),
            in_specs=[
                pl.BlockSpec((parts, count, depth), lambda i, _: (0, 0, 0)),
                weight_spec,
                weight_spec,
            ],
            out_specs=pl.BlockSpec((parts, 1, 2 * height, count), lambda i, _: (0, i, 0, 0)),
            scratch_shapes=[pltpu.VMEM((depth, parts * count), jnp.bfloat16)],
        ),
        out_shape=jax.ShapeDtypeStruct((parts, steps, 2 * height, count), jnp.bfloat16),
        compiler_params=pltpu.CompilerParams(vmem_limit_bytes=24 * MIB),
    )(place, rows, own, other)


def merge_kernel(grad_ref, input_ref, resid_ref, gain_ref, stat_ref, weight_ref, out_ref, handoff):
    count = grad_ref.shape[1]

    @pl.when(pl.program_id(0) == 0)
    def _():
        stats = jnp.sum(stat_ref[...], axis=0)
        inverse = lax.rsqrt(stats[0:1] / D + NORM_EPS)
        factor = inverse * inverse * inverse * stats[1:2] / D
        scaled = gain_ref[...] * grad_ref[...].astype(jnp.float32)
        handoff[...] = (
            resid_ref[...].astype(jnp.float32)
            + inverse * scaled
            - input_ref[...].astype(jnp.float32) * factor
        ).astype(jnp.bfloat16)

    for part in range(out_ref.shape[0]):
        for half in range(2):
            product = jnp.dot(
                weight_ref[2 * part + half], handoff[...], preferred_element_type=jnp.float32
            )
            out_ref[part, :, half * count : (half + 1) * count] = product.astype(out_ref.dtype)


def merge_products(grad, inputs, residual, gain, stats, weights, shares, steps):
    blocks, height, width = weights.shape
    count = grad.shape[1]
    whole = [grad, inputs, residual, gain, stats]
    return pl.pallas_call(
        merge_kernel,
        grid=(steps,),
        in_specs=[
            pl.BlockSpec(a.shape, lambda i, rank=a.ndim: (0,) * rank) for a in whole
        ]
        + [pl.BlockSpec((blocks // steps, height, width), lambda i: (i, 0, 0))],
        out_specs=pl.BlockSpec((shares // steps, height, 2 * count), lambda i: (i, 0, 0)),
        out_shape=jax.ShapeDtypeStruct((shares, height, 2 * count), jnp.bfloat16),
        scratch_shapes=[pltpu.VMEM((width, count), jnp.bfloat16)],
        compiler_params=pltpu.CompilerParams(vmem_limit_bytes=24 * MIB),
    )(*whole, weights)


def send_kernel(hidden_ref, target_ref, out_ref):
    count = target_ref.shape[1]
    total = jnp.sum(hidden_ref[...].astype(jnp.float32), axis=0).astype(jnp.bfloat16)
    spare = out_ref.shape[1] - 2 * total.shape[0]
    columns = jnp.concatenate(
        [total[:, :count], total[:, count:], jnp.zeros((spare, count), jnp.bfloat16)], axis=0
    )
    row = lax.broadcasted_iota(jnp.int32, (out_ref.shape[0], count), 0)
    hot = (row == target_ref[...]).astype(jnp.bfloat16)
    out_ref[...] = lax.dot_general(
        hot, columns, (((1,), (1,)), ((), ())), preferred_element_type=jnp.float32
    ).astype(out_ref.dtype)


def finish_kernel(box_ref, spot_ref, slope_ref, out_ref):
    rows, columns = out_ref.shape
    spot = lax.broadcasted_iota(jnp.int32, (rows, box_ref.shape[0]), 1)
    hot = (spot == spot_ref[...]).astype(jnp.bfloat16)
    hidden = jnp.dot(hot, box_ref[...], preferred_element_type=jnp.float32)
    out_ref[...] = hidden[:, :columns] * slope_ref[...]


def local(
    grad_query,
    query_weight,
    grad_resid,
    embeds,
    norm_gain,
    img_pos,
    img_count,
    img_dest,
    merge_weight,
    merge_pre,
):
    groups = lax.axis_size(DP)
    shares = lax.axis_size(TP)
    side = lax.axis_size("zh")
    rows, columns = merge_pre.shape
    capacity = rows // groups
    positions = img_pos[0]
    image_count = positions.shape[0]

    merge_full = lax.all_gather(merge_weight, DP, axis=0)
    own = lax.all_to_all(
        jnp.broadcast_to(query_weight[None], (side,) + query_weight.shape), "zl", 0, 0, tiled=True
    )
    picked = jnp.take(grad_query, positions, axis=0, mode="clip")
    own, picked = lax.optimization_barrier((own, picked))
    other = lax.ppermute(own, "core", [(0, 1), (1, 0)])
    picked = lax.all_gather(picked, "zh", axis=0)
    inputs = jnp.take(embeds, positions, axis=0, mode="clip").T
    residual = jnp.take(grad_resid, positions, axis=0, mode="clip").T
    gain = norm_gain[:, None]
    wide = inputs.astype(jnp.float32)
    squares = jnp.sum(wide * wide, axis=0)
    is_live = jnp.arange(image_count, dtype=jnp.int32) < img_count[0]
    target_dev = img_dest[0]
    dest_hot = (
        (target_dev[:, None] == jnp.arange(groups, dtype=jnp.int32)[None, :]) & is_live[:, None]
    ).astype(jnp.int32)
    earlier = jnp.cumsum(dest_hot, axis=0) - dest_hot
    slot_index = jnp.sum(earlier * dest_hot, axis=1)
    target = jnp.where(is_live, target_dev * SLOT_PITCH + slot_index, -1)
    number = jnp.arange(rows, dtype=jnp.int32)
    spot = number // capacity * SLOT_PITCH + number % capacity
    slope = gelu_slope(merge_pre)

    place = jnp.stack([lax.axis_index("core"), lax.axis_index("zh")]).astype(jnp.int32)
    partial_value = query_products(place, picked, own, other)
    partial_value = partial_value.reshape((shares,) + partial_value.shape[2:])
    swapped = lax.all_to_all(partial_value, TP, 0, 0, tiled=True)
    normal_grad = jnp.sum(swapped.astype(jnp.float32), axis=0).astype(jnp.bfloat16)
    exchange = [
        (h * side + (a + h) % side, a * side + h) for a in range(side) for h in range(side)
    ]
    normal_grad, merge_full = lax.optimization_barrier((normal_grad, merge_full))
    normal_grad = lax.ppermute(normal_grad, ("zh", "x"), exchange)
    inner = jnp.sum(gain * normal_grad.astype(jnp.float32) * wide, axis=0)
    stats = jnp.stack([squares, inner])
    stats = lax.all_to_all(
        jnp.broadcast_to(stats[None], (shares,) + stats.shape), TP, 0, 0, tiled=True
    )
    partial_hidden = merge_products(
        normal_grad, inputs, residual, gain, stats, merge_full, shares, 4
    )
    hidden = lax.all_to_all(partial_hidden, TP, 0, 0, tiled=True)
    lanes = -(-columns // LANES) * LANES
    outbox = pl.pallas_call(
        send_kernel,
        out_shape=jax.ShapeDtypeStruct((groups * SLOT_PITCH, lanes), jnp.bfloat16),
        compiler_params=pltpu.CompilerParams(vmem_limit_bytes=24 * MIB),
    )(hidden, target[None])
    received = lax.all_to_all(outbox.reshape(groups, SLOT_PITCH, lanes), DP, 0, 0, tiled=True)
    return pl.pallas_call(
        finish_kernel,
        out_shape=jax.ShapeDtypeStruct((rows, columns), jnp.float32),
        compiler_params=pltpu.CompilerParams(vmem_limit_bytes=24 * MIB),
    )(received.reshape(groups * SLOT_PITCH, lanes), spot[:, None], slope)


def solution(mesh):
    split = Mesh(mesh.devices.reshape(4, 4, 2, 4, 4), DP + TP)
    in_specs = (
        P(DP, TP),
        P(DP, TP),
        P(DP, TP),
        P(DP, TP),
        P(TP),
        P(DP, None),
        P(DP),
        P(DP, None),
        P(DP, TP),
        P(DP, TP),
    )
    out_specs = P(DP, TP)
    return jax.shard_map(local, mesh=split, in_specs=in_specs, out_specs=out_specs, check_vma=False)
```

```python
import jax
import jax.numpy as jnp
from jax import lax
from jax.experimental import pallas as pl
from jax.experimental.pallas import tpu as pltpu
from jax.sharding import Mesh
from jax.sharding import PartitionSpec as P

D = 8192
NORM_EPS = 1e-06
MIB = 1024 * 1024
LANES = 128
SLOT_PITCH = 8
DP = ("zh", "zl", "core")
TP = ("x", "y")


def gelu_slope(pre):
    value = pre.astype(jnp.float32)
    cdf_part = 0.5 * (1.0 + lax.erf(value * 0.7071067811865476))
    pdf_part = jnp.exp(-0.5 * value * value) * 0.3989422804014327
    return cdf_part + value * pdf_part


def query_kernel(place_ref, rows_ref, own_ref, other_ref, out_ref):
    parts, count, depth = rows_ref.shape
    blocks, height, _ = own_ref.shape
    core, shift = place_ref[0], place_ref[1]
    turned = rows_ref[...].reshape(parts * count, depth).T
    for block in range(blocks):
        for weight_ref, place in ((own_ref, core), (other_ref, 1 - core)):
            product = jnp.dot(weight_ref[block], turned, preferred_element_type=jnp.float32)
            product = product.astype(out_ref.dtype)
            spot = pl.ds(pl.multiple_of(place * height, height), height)
            for part in range(parts):
                out_ref[lax.rem(part + shift, parts), block, spot] = product[
                    :, part * count : (part + 1) * count
                ]


def query_products(place, rows, own, other):
    parts, count, _ = rows.shape
    blocks, height, _ = own.shape
    return pl.pallas_call(
        query_kernel,
        in_specs=[pl.BlockSpec(memory_space=pltpu.SMEM)]
        + [pl.BlockSpec(memory_space=pltpu.VMEM)] * 3,
        out_specs=pl.BlockSpec(memory_space=pltpu.VMEM),
        out_shape=jax.ShapeDtypeStruct((parts, blocks, 2 * height, count), jnp.bfloat16),
        compiler_params=pltpu.CompilerParams(vmem_limit_bytes=24 * MIB),
    )(place, rows, own, other)


def merge_kernel(grad_ref, input_ref, resid_ref, gain_ref, stat_ref, weight_ref, out_ref):
    count = grad_ref.shape[1]
    stats = jnp.sum(stat_ref[...], axis=0)
    inverse = lax.rsqrt(stats[0:1] / D + NORM_EPS)
    factor = inverse * inverse * inverse * stats[1:2] / D
    scaled = gain_ref[...] * grad_ref[...].astype(jnp.float32)
    handoff = (
        resid_ref[...].astype(jnp.float32)
        + inverse * scaled
        - input_ref[...].astype(jnp.float32) * factor
    ).astype(jnp.bfloat16)
    for share in range(out_ref.shape[0]):
        for half in range(2):
            product = jnp.dot(
                weight_ref[2 * share + half], handoff, preferred_element_type=jnp.float32
            )
            out_ref[share, :, half * count : (half + 1) * count] = product.astype(out_ref.dtype)


def merge_products(grad, inputs, residual, gain, stats, weights, shares):
    _, height, _ = weights.shape
    count = grad.shape[1]
    return pl.pallas_call(
        merge_kernel,
        in_specs=[pl.BlockSpec(memory_space=pltpu.VMEM)] * 6,
        out_specs=pl.BlockSpec(memory_space=pltpu.VMEM),
        out_shape=jax.ShapeDtypeStruct((shares, height, 2 * count), jnp.bfloat16),
        compiler_params=pltpu.CompilerParams(vmem_limit_bytes=24 * MIB),
    )(grad, inputs, residual, gain, stats, weights)


def send_kernel(hidden_ref, target_ref, out_ref):
    count = target_ref.shape[1]
    total = jnp.sum(hidden_ref[...].astype(jnp.float32), axis=0).astype(jnp.bfloat16)
    spare = out_ref.shape[1] - 2 * total.shape[0]
    columns = jnp.concatenate(
        [total[:, :count], total[:, count:], jnp.zeros((spare, count), jnp.bfloat16)], axis=0
    )
    row = lax.broadcasted_iota(jnp.int32, (out_ref.shape[0], count), 0)
    hot = (row == target_ref[...]).astype(jnp.bfloat16)
    out_ref[...] = lax.dot_general(
        hot, columns, (((1,), (1,)), ((), ())), preferred_element_type=jnp.float32
    ).astype(out_ref.dtype)


def finish_kernel(box_ref, spot_ref, slope_ref, out_ref):
    rows, columns = out_ref.shape
    spot = lax.broadcasted_iota(jnp.int32, (rows, box_ref.shape[0]), 1)
    hot = (spot == spot_ref[...]).astype(jnp.bfloat16)
    hidden = jnp.dot(hot, box_ref[...], preferred_element_type=jnp.float32)
    out_ref[...] = hidden[:, :columns] * slope_ref[...]


def local(
    grad_query,
    query_weight,
    grad_resid,
    embeds,
    norm_gain,
    img_pos,
    img_count,
    img_dest,
    merge_weight,
    merge_pre,
):
    groups = lax.axis_size(DP)
    shares = lax.axis_size(TP)
    side = lax.axis_size("zh")
    rows, columns = merge_pre.shape
    capacity = rows // groups
    positions = img_pos[0]
    image_count = positions.shape[0]

    own = lax.all_to_all(
        jnp.broadcast_to(query_weight[None], (side,) + query_weight.shape), "zl", 0, 0, tiled=True
    )
    picked = jnp.take(grad_query, positions, axis=0, mode="clip")
    own, picked, merge_weight = lax.optimization_barrier((own, picked, merge_weight))
    merge_full = lax.all_gather(merge_weight, DP, axis=0)
    other = lax.ppermute(own, "core", [(0, 1), (1, 0)])
    picked = lax.all_gather(picked, "zh", axis=0)
    inputs = jnp.take(embeds, positions, axis=0, mode="clip").T
    residual = jnp.take(grad_resid, positions, axis=0, mode="clip").T
    gain = norm_gain[:, None]
    wide = inputs.astype(jnp.float32)
    squares = jnp.sum(wide * wide, axis=0)
    is_live = jnp.arange(image_count, dtype=jnp.int32) < img_count[0]
    target_dev = img_dest[0]
    dest_hot = (
        (target_dev[:, None] == jnp.arange(groups, dtype=jnp.int32)[None, :]) & is_live[:, None]
    ).astype(jnp.int32)
    earlier = jnp.cumsum(dest_hot, axis=0) - dest_hot
    slot_index = jnp.sum(earlier * dest_hot, axis=1)
    target = jnp.where(is_live, target_dev * SLOT_PITCH + slot_index, -1)
    number = jnp.arange(rows, dtype=jnp.int32)
    spot = number // capacity * SLOT_PITCH + number % capacity
    slope = gelu_slope(merge_pre)

    place = jnp.stack([lax.axis_index("core"), lax.axis_index("zh")]).astype(jnp.int32)
    partial_value = query_products(place, picked, own, other)
    partial_value = partial_value.reshape((shares,) + partial_value.shape[2:])
    swapped = lax.all_to_all(partial_value, TP, 0, 0, tiled=True)
    normal_grad = jnp.sum(swapped.astype(jnp.float32), axis=0).astype(jnp.bfloat16)
    exchange = [
        (h * side + (a + h) % side, a * side + h) for a in range(side) for h in range(side)
    ]
    normal_grad, merge_full = lax.optimization_barrier((normal_grad, merge_full))
    normal_grad = lax.ppermute(normal_grad, ("zh", "x"), exchange)
    inner = jnp.sum(gain * normal_grad.astype(jnp.float32) * wide, axis=0)
    stats = jnp.stack([squares, inner])
    stats = lax.all_to_all(
        jnp.broadcast_to(stats[None], (shares,) + stats.shape), TP, 0, 0, tiled=True
    )
    partial_hidden = merge_products(
        normal_grad, inputs, residual, gain, stats, merge_full, shares
    )
    hidden = lax.all_to_all(partial_hidden, TP, 0, 0, tiled=True)
    lanes = -(-columns // LANES) * LANES
    outbox = pl.pallas_call(
        send_kernel,
        out_shape=jax.ShapeDtypeStruct((groups * SLOT_PITCH, lanes), jnp.bfloat16),
        compiler_params=pltpu.CompilerParams(vmem_limit_bytes=24 * MIB),
    )(hidden, target[None])
    received = lax.all_to_all(outbox.reshape(groups, SLOT_PITCH, lanes), DP, 0, 0, tiled=True)
    return pl.pallas_call(
        finish_kernel,
        out_shape=jax.ShapeDtypeStruct((rows, columns), jnp.float32),
        compiler_params=pltpu.CompilerParams(vmem_limit_bytes=24 * MIB),
    )(received.reshape(groups * SLOT_PITCH, lanes), spot[:, None], slope)


def solution(mesh):
    split = Mesh(mesh.devices.reshape(4, 4, 2, 4, 4), DP + TP)
    in_specs = (
        P(DP, TP),
        P(DP, TP),
        P(DP, TP),
        P(DP, TP),
        P(TP),
        P(DP, None),
        P(DP),
        P(DP, None),
        P(DP, TP),
        P(DP, TP),
    )
    out_specs = P(DP, TP)
    return jax.shard_map(local, mesh=split, in_specs=in_specs, out_specs=out_specs, check_vma=False)
```

```python
import functools

import jax
import jax.numpy as jnp
from jax import lax
from jax.experimental import pallas as pl
from jax.experimental.pallas import tpu as pltpu
from jax.sharding import Mesh
from jax.sharding import PartitionSpec as P

D = 8192
NORM_EPS = 1e-06
MIB = 1024 * 1024
LANES = 128
DP = ("zh", "zl", "core")
TP = ("x", "y")


def gelu_slope(pre):
    value = pre.astype(jnp.float32)
    cdf_part = 0.5 * (1.0 + lax.erf(value * 0.7071067811865476))
    pdf_part = jnp.exp(-0.5 * value * value) * 0.3989422804014327
    return cdf_part + value * pdf_part


def own_kernel(rows_ref, weight_ref, out_ref, turned_ref):
    parts, count, depth = rows_ref.shape
    turned_ref[...] = rows_ref[...].reshape(parts * count, depth).T
    for block in range(weight_ref.shape[0]):
        product = jnp.dot(weight_ref[block], turned_ref[...], preferred_element_type=jnp.float32)
        out_ref[block] = product.astype(out_ref.dtype)


def join_kernel(place_ref, own_ref, turned_ref, weight_ref, out_ref):
    parts, blocks, _, count = out_ref.shape
    height = weight_ref.shape[1]
    core, shift = place_ref[0], place_ref[1]
    spots = [
        pl.ds(pl.multiple_of(place * height, height), height) for place in (core, 1 - core)
    ]
    for block in range(blocks):
        product = jnp.dot(weight_ref[block], turned_ref[...], preferred_element_type=jnp.float32)
        halves = (own_ref[block], product.astype(out_ref.dtype))
        for spot, half in zip(spots, halves):
            for part in range(parts):
                out_ref[lax.rem(part + shift, parts), block, spot] = half[
                    :, part * count : (part + 1) * count
                ]


def in_vmem(kernel, out_shape, *args, scalars=False):
    specs = [pl.BlockSpec(memory_space=pltpu.VMEM) for _ in args]
    if scalars:
        specs[0] = pl.BlockSpec(memory_space=pltpu.SMEM)
    return pl.pallas_call(
        kernel,
        in_specs=specs,
        out_specs=jax.tree.map(lambda _: pl.BlockSpec(memory_space=pltpu.VMEM), out_shape),
        out_shape=out_shape,
        compiler_params=pltpu.CompilerParams(vmem_limit_bytes=24 * MIB),
    )(*args)


def stat_kernel(grad_ref, scaled_ref, square_ref, out_ref):
    inner = jnp.sum(
        grad_ref[...].astype(jnp.float32) * scaled_ref[...], axis=0, keepdims=True
    )
    stats = jnp.concatenate([square_ref[...], inner], axis=0)
    for share in range(out_ref.shape[0]):
        out_ref[share] = stats


def handoff_kernel(capacity, grad_ref, input_ref, resid_ref, gain_ref, stat_ref, target_ref, out_ref):
    width, count = grad_ref.shape
    stats = jnp.sum(stat_ref[...], axis=0)
    inverse = lax.rsqrt(stats[0:1] / D + NORM_EPS)
    factor = inverse * inverse * inverse * stats[1:2] / D
    scaled = gain_ref[...] * grad_ref[...].astype(jnp.float32)
    handoff = (
        resid_ref[...].astype(jnp.float32)
        + inverse * scaled
        - input_ref[...].astype(jnp.float32) * factor
    ).astype(jnp.bfloat16)
    place = lax.broadcasted_iota(jnp.int32, (out_ref.shape[0], count), 0) - target_ref[...]
    total = jnp.zeros(out_ref.shape, jnp.float32)
    for block in range(width // LANES):
        hot = (place == block * capacity).astype(jnp.bfloat16)
        total += lax.dot_general(
            hot,
            handoff[block * LANES : (block + 1) * LANES],
            (((1,), (1,)), ((), ())),
            preferred_element_type=jnp.float32,
        )
    out_ref[...] = total.astype(out_ref.dtype)


def merge_kernel(capacity, box_ref, weight_ref, out_ref):
    width = weight_ref.shape[2]
    rows = out_ref.shape[2] // 2
    chunks = width // LANES
    box = box_ref[...]
    row = lax.broadcasted_iota(jnp.int32, (rows, box.shape[0]), 0)
    spot = lax.broadcasted_iota(jnp.int32, (rows, box.shape[0]), 1)
    source = (row * 10923) >> 16
    ahead = spot - (row + source * (capacity * (chunks - 1)))
    pieces = []
    for block in range(chunks):
        hot = (ahead == block * capacity).astype(jnp.bfloat16)
        piece = jnp.dot(hot, box, preferred_element_type=jnp.float32)
        pieces.append(piece.T.astype(jnp.bfloat16))
    turned = jnp.concatenate(pieces, axis=0)
    for share in range(out_ref.shape[0]):
        for half in range(2):
            product = jnp.dot(
                weight_ref[2 * share + half], turned, preferred_element_type=jnp.float32
            )
            out_ref[share, :, half * rows : (half + 1) * rows] = product.astype(out_ref.dtype)


def local(
    grad_query,
    query_weight,
    grad_resid,
    embeds,
    norm_gain,
    img_pos,
    img_count,
    img_dest,
    merge_weight,
    merge_pre,
):
    groups = lax.axis_size(DP)
    shares = lax.axis_size(TP)
    side = lax.axis_size("zh")
    rows, columns = merge_pre.shape
    capacity = rows // groups
    positions = img_pos[0]
    image_count = positions.shape[0]
    width = embeds.shape[1]

    own = lax.all_gather(query_weight, "zl", axis=0)
    picked = lax.all_gather(jnp.take(grad_query, positions, axis=0, mode="clip"), "zh", axis=0)
    merge_weight, picked = lax.optimization_barrier((merge_weight, picked))
    merge_full = lax.all_gather(merge_weight, DP, axis=0)
    inputs = jnp.take(embeds, positions, axis=0, mode="clip").T
    residual = jnp.take(grad_resid, positions, axis=0, mode="clip").T
    gain = norm_gain[:, None]
    wide = inputs.astype(jnp.float32)
    squares = jnp.sum(wide * wide, axis=0)
    is_live = jnp.arange(image_count, dtype=jnp.int32) < img_count[0]
    target_dev = img_dest[0]
    dest_hot = (
        (target_dev[:, None] == jnp.arange(groups, dtype=jnp.int32)[None, :]) & is_live[:, None]
    ).astype(jnp.int32)
    earlier = jnp.cumsum(dest_hot, axis=0) - dest_hot
    slot_index = jnp.sum(earlier * dest_hot, axis=1)
    pitch = capacity * (width // LANES)
    target = jnp.where(is_live, target_dev * pitch + slot_index, -groups * pitch)
    slope = gelu_slope(merge_pre)

    other = lax.ppermute(own, "core", [(0, 1), (1, 0)])
    place = jnp.stack([lax.axis_index("core"), lax.axis_index("zh")]).astype(jnp.int32)
    blocks, height, depth = own.shape
    own_value, turned = in_vmem(
        own_kernel,
        [
            jax.ShapeDtypeStruct((blocks, height, side * image_count), jnp.bfloat16),
            jax.ShapeDtypeStruct((depth, side * image_count), jnp.bfloat16),
        ],
        picked,
        own,
    )
    partial_value = in_vmem(
        join_kernel,
        jax.ShapeDtypeStruct((side, blocks, 2 * height, image_count), jnp.bfloat16),
        place,
        own_value,
        turned,
        other,
        scalars=True,
    )
    partial_value = partial_value.reshape(shares, width, image_count)
    swapped = lax.all_to_all(partial_value, TP, 0, 0, tiled=True)
    normal_grad = jnp.sum(swapped.astype(jnp.float32), axis=0).astype(jnp.bfloat16)
    exchange = [
        (h * side + (a + h) % side, a * side + h) for a in range(side) for h in range(side)
    ]
    normal_grad = lax.ppermute(normal_grad, ("zh", "x"), exchange)
    stats = in_vmem(
        stat_kernel,
        jax.ShapeDtypeStruct((shares, 2, image_count), jnp.float32),
        normal_grad,
        gain * wide,
        squares[None],
    )
    stats = lax.all_to_all(stats, TP, 0, 0, tiled=True)
    outbox = in_vmem(
        functools.partial(handoff_kernel, capacity),
        jax.ShapeDtypeStruct((groups * pitch, LANES), jnp.bfloat16),
        normal_grad,
        inputs,
        residual,
        gain,
        stats,
        target[None],
    )
    received = lax.all_to_all(outbox.reshape(groups, pitch, LANES), DP, 0, 0, tiled=True)
    partial_hidden = in_vmem(
        functools.partial(merge_kernel, capacity),
        jax.ShapeDtypeStruct((shares, merge_weight.shape[0], 2 * rows), jnp.bfloat16),
        received.reshape(groups * pitch, LANES),
        merge_full,
    )
    hidden = lax.all_to_all(partial_hidden, TP, 0, 0, tiled=True)
    hidden = jnp.sum(hidden.astype(jnp.float32), axis=0)
    hidden = jnp.concatenate([hidden[:, :rows].T, hidden[:, rows:].T], axis=1)
    return hidden * slope


def solution(mesh):
    split = Mesh(mesh.devices.reshape(4, 4, 2, 4, 4), DP + TP)
    in_specs = (
        P(DP, TP),
        P(DP, TP),
        P(DP, TP),
        P(DP, TP),
        P(TP),
        P(DP, None),
        P(DP),
        P(DP, None),
        P(DP, TP),
        P(DP, TP),
    )
    out_specs = P(DP, TP)
    return jax.shard_map(local, mesh=split, in_specs=in_specs, out_specs=out_specs, check_vma=False)
```

```python
import functools

import jax
import jax.numpy as jnp
from jax import lax
from jax.experimental import pallas as pl
from jax.experimental.pallas import tpu as pltpu
from jax.sharding import Mesh
from jax.sharding import PartitionSpec as P

D = 8192
NORM_EPS = 1e-06
MIB = 1024 * 1024
LANES = 128
DP = ("zh", "zl", "core")
TP = ("x", "y")


def gelu_slope(pre):
    value = pre.astype(jnp.float32)
    cdf_part = 0.5 * (1.0 + lax.erf(value * 0.7071067811865476))
    pdf_part = jnp.exp(-0.5 * value * value) * 0.3989422804014327
    return cdf_part + value * pdf_part


def own_kernel(rows_ref, weight_ref, out_ref, turned_ref):
    parts, count, depth = rows_ref.shape
    turned_ref[...] = rows_ref[...].reshape(parts * count, depth).T
    for block in range(weight_ref.shape[0]):
        product = jnp.dot(weight_ref[block], turned_ref[...], preferred_element_type=jnp.float32)
        out_ref[block] = product.astype(out_ref.dtype)


def join_kernel(place_ref, own_ref, turned_ref, weight_ref, out_ref):
    parts, blocks, _, count = out_ref.shape
    height = weight_ref.shape[1]
    core, shift = place_ref[0], place_ref[1]
    spots = [
        pl.ds(pl.multiple_of(place * height, height), height) for place in (core, 1 - core)
    ]
    for block in range(blocks):
        product = jnp.dot(weight_ref[block], turned_ref[...], preferred_element_type=jnp.float32)
        halves = (own_ref[block], product.astype(out_ref.dtype))
        for spot, half in zip(spots, halves):
            for part in range(parts):
                out_ref[lax.rem(part + shift, parts), block, spot] = half[
                    :, part * count : (part + 1) * count
                ]


def in_vmem(kernel, out_shape, *args, scalars=False):
    specs = [pl.BlockSpec(memory_space=pltpu.VMEM) for _ in args]
    if scalars:
        specs[0] = pl.BlockSpec(memory_space=pltpu.SMEM)
    return pl.pallas_call(
        kernel,
        in_specs=specs,
        out_specs=jax.tree.map(lambda _: pl.BlockSpec(memory_space=pltpu.VMEM), out_shape),
        out_shape=out_shape,
        compiler_params=pltpu.CompilerParams(vmem_limit_bytes=24 * MIB),
    )(*args)


def stat_kernel(grad_ref, scaled_ref, square_ref, out_ref):
    inner = jnp.sum(
        grad_ref[...].astype(jnp.float32) * scaled_ref[...], axis=0, keepdims=True
    )
    stats = jnp.concatenate([square_ref[...], inner], axis=0)
    for share in range(out_ref.shape[0]):
        out_ref[share] = stats


def handoff_kernel(capacity, grad_ref, input_ref, resid_ref, gain_ref, stat_ref, target_ref, out_ref):
    width, count = grad_ref.shape
    stats = jnp.sum(stat_ref[...], axis=0)
    inverse = lax.rsqrt(stats[0:1] / D + NORM_EPS)
    factor = inverse * inverse * inverse * stats[1:2] / D
    scaled = gain_ref[...] * grad_ref[...].astype(jnp.float32)
    handoff = (
        resid_ref[...].astype(jnp.float32)
        + inverse * scaled
        - input_ref[...].astype(jnp.float32) * factor
    ).astype(jnp.bfloat16)
    place = lax.broadcasted_iota(jnp.int32, (out_ref.shape[0], count), 0) - target_ref[...]
    total = jnp.zeros(out_ref.shape, jnp.float32)
    for block in range(width // LANES):
        hot = (place == block * capacity).astype(jnp.bfloat16)
        total += lax.dot_general(
            hot,
            handoff[block * LANES : (block + 1) * LANES],
            (((1,), (1,)), ((), ())),
            preferred_element_type=jnp.float32,
        )
    out_ref[...] = total.astype(out_ref.dtype)


def merge_kernel(capacity, box_ref, weight_ref, out_ref):
    width = weight_ref.shape[2]
    rows = out_ref.shape[2] // 2
    chunks = width // LANES
    box = box_ref[...]
    row = lax.broadcasted_iota(jnp.int32, (rows, box.shape[0]), 0)
    spot = lax.broadcasted_iota(jnp.int32, (rows, box.shape[0]), 1)
    source = (row * 10923) >> 16
    ahead = spot - (row + source * (capacity * (chunks - 1)))
    pieces = []
    for block in range(chunks):
        hot = (ahead == block * capacity).astype(jnp.bfloat16)
        piece = jnp.dot(hot, box, preferred_element_type=jnp.float32)
        pieces.append(piece.T.astype(jnp.bfloat16))
    turned = jnp.concatenate(pieces, axis=0)
    for share in range(out_ref.shape[0]):
        for half in range(2):
            product = jnp.dot(
                weight_ref[2 * share + half], turned, preferred_element_type=jnp.float32
            )
            out_ref[share, :, half * rows : (half + 1) * rows] = product.astype(out_ref.dtype)


def local(
    grad_query,
    query_weight,
    grad_resid,
    embeds,
    norm_gain,
    img_pos,
    img_count,
    img_dest,
    merge_weight,
    merge_pre,
):
    groups = lax.axis_size(DP)
    shares = lax.axis_size(TP)
    side = lax.axis_size("zh")
    rows, columns = merge_pre.shape
    capacity = rows // groups
    positions = img_pos[0]
    image_count = positions.shape[0]
    width = embeds.shape[1]

    own = lax.all_gather(query_weight, "zl", axis=0)
    picked = lax.all_gather(jnp.take(grad_query, positions, axis=0, mode="clip"), "zh", axis=0)
    merge_weight, embeds, grad_resid, img_dest, merge_pre, picked = lax.optimization_barrier(
        (merge_weight, embeds, grad_resid, img_dest, merge_pre, picked)
    )
    merge_full = lax.all_gather(merge_weight, DP, axis=0)
    inputs = jnp.take(embeds, positions, axis=0, mode="clip").T
    residual = jnp.take(grad_resid, positions, axis=0, mode="clip").T
    gain = norm_gain[:, None]
    wide = inputs.astype(jnp.float32)
    squares = jnp.sum(wide * wide, axis=0)
    is_live = jnp.arange(image_count, dtype=jnp.int32) < img_count[0]
    target_dev = img_dest[0]
    dest_hot = (
        (target_dev[:, None] == jnp.arange(groups, dtype=jnp.int32)[None, :]) & is_live[:, None]
    ).astype(jnp.int32)
    earlier = jnp.cumsum(dest_hot, axis=0) - dest_hot
    slot_index = jnp.sum(earlier * dest_hot, axis=1)
    pitch = capacity * (width // LANES)
    target = jnp.where(is_live, target_dev * pitch + slot_index, -groups * pitch)
    slope = gelu_slope(merge_pre)

    scaled_input = gain * wide
    own, picked, inputs, residual, gain, squares, scaled_input, target, slope = (
        lax.optimization_barrier(
            (own, picked, inputs, residual, gain, squares, scaled_input, target, slope)
        )
    )
    other = lax.ppermute(own, "core", [(0, 1), (1, 0)])
    place = jnp.stack([lax.axis_index("core"), lax.axis_index("zh")]).astype(jnp.int32)
    blocks, height, depth = own.shape
    own_value, turned = in_vmem(
        own_kernel,
        [
            jax.ShapeDtypeStruct((blocks, height, side * image_count), jnp.bfloat16),
            jax.ShapeDtypeStruct((depth, side * image_count), jnp.bfloat16),
        ],
        picked,
        own,
    )
    partial_value = in_vmem(
        join_kernel,
        jax.ShapeDtypeStruct((side, blocks, 2 * height, image_count), jnp.bfloat16),
        place,
        own_value,
        turned,
        other,
        scalars=True,
    )
    partial_value = partial_value.reshape(shares, width, image_count)
    swapped = lax.all_to_all(partial_value, TP, 0, 0, tiled=True)
    normal_grad = jnp.sum(swapped.astype(jnp.float32), axis=0).astype(jnp.bfloat16)
    exchange = [
        (h * side + (a + h) % side, a * side + h) for a in range(side) for h in range(side)
    ]
    normal_grad = lax.ppermute(normal_grad, ("zh", "x"), exchange)
    stats = in_vmem(
        stat_kernel,
        jax.ShapeDtypeStruct((shares, 2, image_count), jnp.float32),
        normal_grad,
        scaled_input,
        squares[None],
    )
    stats = lax.all_to_all(stats, TP, 0, 0, tiled=True)
    outbox = in_vmem(
        functools.partial(handoff_kernel, capacity),
        jax.ShapeDtypeStruct((groups * pitch, LANES), jnp.bfloat16),
        normal_grad,
        inputs,
        residual,
        gain,
        stats,
        target[None],
    )
    received = lax.all_to_all(outbox.reshape(groups, pitch, LANES), DP, 0, 0, tiled=True)
    partial_hidden = in_vmem(
        functools.partial(merge_kernel, capacity),
        jax.ShapeDtypeStruct((shares, merge_weight.shape[0], 2 * rows), jnp.bfloat16),
        received.reshape(groups * pitch, LANES),
        merge_full,
    )
    hidden = lax.all_to_all(partial_hidden, TP, 0, 0, tiled=True)
    hidden = jnp.sum(hidden.astype(jnp.float32), axis=0)
    hidden = jnp.concatenate([hidden[:, :rows].T, hidden[:, rows:].T], axis=1)
    return hidden * slope


def solution(mesh):
    split = Mesh(mesh.devices.reshape(4, 4, 2, 4, 4), DP + TP)
    in_specs = (
        P(DP, TP),
        P(DP, TP),
        P(DP, TP),
        P(DP, TP),
        P(TP),
        P(DP, None),
        P(DP),
        P(DP, None),
        P(DP, TP),
        P(DP, TP),
    )
    out_specs = P(DP, TP)
    return jax.shard_map(local, mesh=split, in_specs=in_specs, out_specs=out_specs, check_vma=False)
```

```python
import functools

import jax
import jax.numpy as jnp
from jax import lax
from jax.experimental import pallas as pl
from jax.experimental.pallas import tpu as pltpu
from jax.sharding import Mesh
from jax.sharding import PartitionSpec as P

D = 8192
NORM_EPS = 1e-06
MIB = 1024 * 1024
LANES = 128
DP = ("zh", "zl", "core")
TP = ("x", "y")


def gelu_slope(pre):
    value = pre.astype(jnp.float32)
    cdf_part = 0.5 * (1.0 + lax.erf(value * 0.7071067811865476))
    pdf_part = jnp.exp(-0.5 * value * value) * 0.3989422804014327
    return cdf_part + value * pdf_part


def own_kernel(rows_ref, weight_ref, out_ref, turned_ref):
    parts, count, depth = rows_ref.shape
    turned_ref[...] = rows_ref[...].reshape(parts * count, depth).T
    for block in range(weight_ref.shape[0]):
        product = jnp.dot(weight_ref[block], turned_ref[...], preferred_element_type=jnp.float32)
        out_ref[block] = product.astype(out_ref.dtype)


def join_kernel(place_ref, own_ref, turned_ref, weight_ref, out_ref):
    parts, blocks, _, count = out_ref.shape
    height = weight_ref.shape[1]
    core, shift = place_ref[0], place_ref[1]
    spots = [
        pl.ds(pl.multiple_of(place * height, height), height) for place in (core, 1 - core)
    ]
    for block in range(blocks):
        product = jnp.dot(weight_ref[block], turned_ref[...], preferred_element_type=jnp.float32)
        halves = (own_ref[block], product.astype(out_ref.dtype))
        for spot, half in zip(spots, halves):
            for part in range(parts):
                out_ref[lax.rem(part + shift, parts), block, spot] = half[
                    :, part * count : (part + 1) * count
                ]


def in_vmem(kernel, out_shape, *args, scalars=False):
    specs = [pl.BlockSpec(memory_space=pltpu.VMEM) for _ in args]
    if scalars:
        specs[0] = pl.BlockSpec(memory_space=pltpu.SMEM)
    return pl.pallas_call(
        kernel,
        in_specs=specs,
        out_specs=jax.tree.map(lambda _: pl.BlockSpec(memory_space=pltpu.VMEM), out_shape),
        out_shape=out_shape,
        compiler_params=pltpu.CompilerParams(vmem_limit_bytes=24 * MIB),
    )(*args)


def pick_kernel(position_ref, source_ref, out_ref):
    count = position_ref.shape[1]
    token = lax.broadcasted_iota(jnp.int32, (source_ref.shape[0], count), 0)
    hot = (token == position_ref[...]).astype(jnp.bfloat16)
    out_ref[...] = lax.dot_general(
        hot, source_ref[...], (((0,), (0,)), ((), ())), preferred_element_type=jnp.float32
    ).astype(out_ref.dtype)


def finish_kernel(hidden_ref, slope_ref, out_ref):
    _, height, double = hidden_ref.shape
    rows = double // 2
    total = hidden_ref[0].astype(jnp.float32)
    for share in range(1, hidden_ref.shape[0]):
        total += hidden_ref[share].astype(jnp.float32)
    for half in range(2):
        piece = total[:, half * rows : (half + 1) * rows].T
        spot = slice(half * height, (half + 1) * height)
        out_ref[:, spot] = piece * slope_ref[:, spot]


def stat_kernel(grad_ref, scaled_ref, square_ref, out_ref):
    inner = jnp.sum(
        grad_ref[...].astype(jnp.float32) * scaled_ref[...], axis=0, keepdims=True
    )
    stats = jnp.concatenate([square_ref[...], inner], axis=0)
    for share in range(out_ref.shape[0]):
        out_ref[share] = stats


def handoff_kernel(capacity, grad_ref, input_ref, resid_ref, gain_ref, stat_ref, target_ref, out_ref):
    width, count = grad_ref.shape
    stats = jnp.sum(stat_ref[...], axis=0)
    inverse = lax.rsqrt(stats[0:1] / D + NORM_EPS)
    factor = inverse * inverse * inverse * stats[1:2] / D
    scaled = gain_ref[...] * grad_ref[...].astype(jnp.float32)
    handoff = (
        resid_ref[...].astype(jnp.float32)
        + inverse * scaled
        - input_ref[...].astype(jnp.float32) * factor
    ).astype(jnp.bfloat16)
    place = lax.broadcasted_iota(jnp.int32, (out_ref.shape[0], count), 0) - target_ref[...]
    total = jnp.zeros(out_ref.shape, jnp.float32)
    for block in range(width // LANES):
        hot = (place == block * capacity).astype(jnp.bfloat16)
        total += lax.dot_general(
            hot,
            handoff[block * LANES : (block + 1) * LANES],
            (((1,), (1,)), ((), ())),
            preferred_element_type=jnp.float32,
        )
    out_ref[...] = total.astype(out_ref.dtype)


def merge_kernel(capacity, box_ref, weight_ref, out_ref):
    width = weight_ref.shape[2]
    rows = out_ref.shape[2] // 2
    chunks = width // LANES
    box = box_ref[...]
    row = lax.broadcasted_iota(jnp.int32, (rows, box.shape[0]), 0)
    spot = lax.broadcasted_iota(jnp.int32, (rows, box.shape[0]), 1)
    source = (row * 10923) >> 16
    ahead = spot - (row + source * (capacity * (chunks - 1)))
    pieces = []
    for block in range(chunks):
        hot = (ahead == block * capacity).astype(jnp.bfloat16)
        piece = jnp.dot(hot, box, preferred_element_type=jnp.float32)
        pieces.append(piece.T.astype(jnp.bfloat16))
    turned = jnp.concatenate(pieces, axis=0)
    for share in range(out_ref.shape[0]):
        for half in range(2):
            product = jnp.dot(
                weight_ref[2 * share + half], turned, preferred_element_type=jnp.float32
            )
            out_ref[share, :, half * rows : (half + 1) * rows] = product.astype(out_ref.dtype)


def local(
    grad_query,
    query_weight,
    grad_resid,
    embeds,
    norm_gain,
    img_pos,
    img_count,
    img_dest,
    merge_weight,
    merge_pre,
):
    groups = lax.axis_size(DP)
    shares = lax.axis_size(TP)
    side = lax.axis_size("zh")
    rows, columns = merge_pre.shape
    capacity = rows // groups
    positions = img_pos[0]
    image_count = positions.shape[0]
    width = embeds.shape[1]

    own = lax.all_gather(query_weight, "zl", axis=0)
    picked = in_vmem(
        pick_kernel,
        jax.ShapeDtypeStruct((image_count, grad_query.shape[1]), jnp.bfloat16),
        img_pos,
        grad_query,
    )
    picked = lax.all_gather(picked, "zh", axis=0)
    merge_weight, embeds, grad_resid, img_dest, picked = lax.optimization_barrier(
        (merge_weight, embeds, grad_resid, img_dest, picked)
    )
    merge_full = lax.all_gather(merge_weight, DP, axis=0)
    inputs = jnp.take(embeds, positions, axis=0, mode="clip").T
    residual = jnp.take(grad_resid, positions, axis=0, mode="clip").T
    gain = norm_gain[:, None]
    wide = inputs.astype(jnp.float32)
    squares = jnp.sum(wide * wide, axis=0)
    is_live = jnp.arange(image_count, dtype=jnp.int32) < img_count[0]
    target_dev = img_dest[0]
    dest_hot = (
        (target_dev[:, None] == jnp.arange(groups, dtype=jnp.int32)[None, :]) & is_live[:, None]
    ).astype(jnp.int32)
    earlier = jnp.cumsum(dest_hot, axis=0) - dest_hot
    slot_index = jnp.sum(earlier * dest_hot, axis=1)
    pitch = capacity * (width // LANES)
    target = jnp.where(is_live, target_dev * pitch + slot_index, -groups * pitch)

    scaled_input = gain * wide
    own, picked, inputs, residual, gain, squares, scaled_input, target = (
        lax.optimization_barrier(
            (own, picked, inputs, residual, gain, squares, scaled_input, target)
        )
    )
    other = lax.ppermute(own, "core", [(0, 1), (1, 0)])
    place = jnp.stack([lax.axis_index("core"), lax.axis_index("zh")]).astype(jnp.int32)
    blocks, height, depth = own.shape
    own_value, turned = in_vmem(
        own_kernel,
        [
            jax.ShapeDtypeStruct((blocks, height, side * image_count), jnp.bfloat16),
            jax.ShapeDtypeStruct((depth, side * image_count), jnp.bfloat16),
        ],
        picked,
        own,
    )
    partial_value = in_vmem(
        join_kernel,
        jax.ShapeDtypeStruct((side, blocks, 2 * height, image_count), jnp.bfloat16),
        place,
        own_value,
        turned,
        other,
        scalars=True,
    )
    partial_value = partial_value.reshape(shares, width, image_count)
    swapped = lax.all_to_all(partial_value, TP, 0, 0, tiled=True)
    normal_grad = jnp.sum(swapped.astype(jnp.float32), axis=0).astype(jnp.bfloat16)
    exchange = [
        (h * side + (a + h) % side, a * side + h) for a in range(side) for h in range(side)
    ]
    normal_grad = lax.ppermute(normal_grad, ("zh", "x"), exchange)
    stats = in_vmem(
        stat_kernel,
        jax.ShapeDtypeStruct((shares, 2, image_count), jnp.float32),
        normal_grad,
        scaled_input,
        squares[None],
    )
    stats = lax.all_to_all(stats, TP, 0, 0, tiled=True)
    outbox = in_vmem(
        functools.partial(handoff_kernel, capacity),
        jax.ShapeDtypeStruct((groups * pitch, LANES), jnp.bfloat16),
        normal_grad,
        inputs,
        residual,
        gain,
        stats,
        target[None],
    )
    outbox, merge_pre = lax.optimization_barrier((outbox, merge_pre))
    slope = gelu_slope(merge_pre)
    received = lax.all_to_all(outbox.reshape(groups, pitch, LANES), DP, 0, 0, tiled=True)
    received, slope = lax.optimization_barrier((received, slope))
    partial_hidden = in_vmem(
        functools.partial(merge_kernel, capacity),
        jax.ShapeDtypeStruct((shares, merge_weight.shape[0], 2 * rows), jnp.bfloat16),
        received.reshape(groups * pitch, LANES),
        merge_full,
    )
    hidden = lax.all_to_all(partial_hidden, TP, 0, 0, tiled=True)
    return in_vmem(
        finish_kernel,
        jax.ShapeDtypeStruct((rows, columns), jnp.float32),
        hidden,
        slope,
    )


def solution(mesh):
    split = Mesh(mesh.devices.reshape(4, 4, 2, 4, 4), DP + TP)
    in_specs = (
        P(DP, TP),
        P(DP, TP),
        P(DP, TP),
        P(DP, TP),
        P(TP),
        P(DP, None),
        P(DP),
        P(DP, None),
        P(DP, TP),
        P(DP, TP),
    )
    out_specs = P(DP, TP)
    return jax.shard_map(local, mesh=split, in_specs=in_specs, out_specs=out_specs, check_vma=False)
```

```python
import functools

import jax
import jax.numpy as jnp
from jax import lax
from jax.experimental import pallas as pl
from jax.experimental.pallas import tpu as pltpu
from jax.sharding import Mesh
from jax.sharding import PartitionSpec as P

D = 8192
NORM_EPS = 1e-06
MIB = 1024 * 1024
LANES = 128
DP = ("zh", "zl", "core")
TP = ("x", "y")


def gelu_slope(pre):
    value = pre.astype(jnp.float32)
    cdf_part = 0.5 * (1.0 + lax.erf(value * 0.7071067811865476))
    pdf_part = jnp.exp(-0.5 * value * value) * 0.3989422804014327
    return cdf_part + value * pdf_part


def own_kernel(rows_ref, weight_ref, out_ref, turned_ref):
    parts, count, depth = rows_ref.shape
    turned_ref[...] = rows_ref[...].reshape(parts * count, depth).T
    for block in range(weight_ref.shape[0]):
        product = jnp.dot(weight_ref[block], turned_ref[...], preferred_element_type=jnp.float32)
        out_ref[block] = product.astype(out_ref.dtype)


def join_kernel(place_ref, own_ref, turned_ref, weight_ref, out_ref):
    parts, blocks, _, count = out_ref.shape
    height = weight_ref.shape[1]
    core, shift = place_ref[0], place_ref[1]
    spots = [
        pl.ds(pl.multiple_of(place * height, height), height) for place in (core, 1 - core)
    ]
    for block in range(blocks):
        product = jnp.dot(weight_ref[block], turned_ref[...], preferred_element_type=jnp.float32)
        halves = (own_ref[block], product.astype(out_ref.dtype))
        for spot, half in zip(spots, halves):
            for part in range(parts):
                out_ref[lax.rem(part + shift, parts), block, spot] = half[
                    :, part * count : (part + 1) * count
                ]


def in_vmem(kernel, out_shape, *args, scalars=False):
    specs = [pl.BlockSpec(memory_space=pltpu.VMEM) for _ in args]
    if scalars:
        specs[0] = pl.BlockSpec(memory_space=pltpu.SMEM)
    return pl.pallas_call(
        kernel,
        in_specs=specs,
        out_specs=jax.tree.map(lambda _: pl.BlockSpec(memory_space=pltpu.VMEM), out_shape),
        out_shape=out_shape,
        compiler_params=pltpu.CompilerParams(vmem_limit_bytes=24 * MIB),
    )(*args)


def finish_kernel(hidden_ref, slope_ref, out_ref):
    _, height, double = hidden_ref.shape
    rows = double // 2
    total = hidden_ref[0].astype(jnp.float32)
    for share in range(1, hidden_ref.shape[0]):
        total += hidden_ref[share].astype(jnp.float32)
    for half in range(2):
        piece = total[:, half * rows : (half + 1) * rows].T
        spot = slice(half * height, (half + 1) * height)
        out_ref[:, spot] = piece * slope_ref[:, spot]


def stat_kernel(grad_ref, scaled_ref, square_ref, out_ref):
    inner = jnp.sum(
        grad_ref[...].astype(jnp.float32) * scaled_ref[...], axis=0, keepdims=True
    )
    stats = jnp.concatenate([square_ref[...], inner], axis=0)
    for share in range(out_ref.shape[0]):
        out_ref[share] = stats


def handoff_kernel(capacity, grad_ref, input_ref, resid_ref, gain_ref, stat_ref, target_ref, out_ref):
    width, count = grad_ref.shape
    stats = jnp.sum(stat_ref[...], axis=0)
    inverse = lax.rsqrt(stats[0:1] / D + NORM_EPS)
    factor = inverse * inverse * inverse * stats[1:2] / D
    equal = lax.broadcasted_iota(jnp.int32, (LANES, LANES), 0) == lax.broadcasted_iota(
        jnp.int32, (LANES, LANES), 1
    )
    gain = jnp.concatenate(
        [
            jnp.sum(
                jnp.where(equal, gain_ref[:, at : at + LANES], 0.0), axis=1, keepdims=True
            )
            for at in range(0, width, LANES)
        ],
        axis=0,
    )
    scaled = gain * grad_ref[...].astype(jnp.float32)
    handoff = (
        resid_ref[...].astype(jnp.float32)
        + inverse * scaled
        - input_ref[...].astype(jnp.float32) * factor
    ).astype(jnp.bfloat16)
    place = lax.broadcasted_iota(jnp.int32, (out_ref.shape[0], count), 0) - target_ref[...]
    total = jnp.zeros(out_ref.shape, jnp.float32)
    for block in range(width // LANES):
        hot = (place == block * capacity).astype(jnp.bfloat16)
        total += lax.dot_general(
            hot,
            handoff[block * LANES : (block + 1) * LANES],
            (((1,), (1,)), ((), ())),
            preferred_element_type=jnp.float32,
        )
    out_ref[...] = total.astype(out_ref.dtype)


def merge_kernel(capacity, box_ref, weight_ref, out_ref):
    width = weight_ref.shape[2]
    rows = out_ref.shape[2] // 2
    chunks = width // LANES
    box = box_ref[...]
    row = lax.broadcasted_iota(jnp.int32, (rows, box.shape[0]), 0)
    spot = lax.broadcasted_iota(jnp.int32, (rows, box.shape[0]), 1)
    source = (row * 10923) >> 16
    ahead = spot - (row + source * (capacity * (chunks - 1)))
    pieces = []
    for block in range(chunks):
        hot = (ahead == block * capacity).astype(jnp.bfloat16)
        piece = jnp.dot(hot, box, preferred_element_type=jnp.float32)
        pieces.append(piece.T.astype(jnp.bfloat16))
    turned = jnp.concatenate(pieces, axis=0)
    for share in range(out_ref.shape[0]):
        for half in range(2):
            product = jnp.dot(
                weight_ref[2 * share + half], turned, preferred_element_type=jnp.float32
            )
            out_ref[share, :, half * rows : (half + 1) * rows] = product.astype(out_ref.dtype)


def local(
    grad_query,
    query_weight,
    grad_resid,
    embeds,
    norm_gain,
    img_pos,
    img_count,
    img_dest,
    merge_weight,
    merge_pre,
):
    groups = lax.axis_size(DP)
    shares = lax.axis_size(TP)
    side = lax.axis_size("zh")
    rows, columns = merge_pre.shape
    capacity = rows // groups
    positions = img_pos[0]
    image_count = positions.shape[0]
    width = embeds.shape[1]

    picked = jnp.take(grad_query, positions, axis=0, mode="clip")
    query_weight, picked = lax.optimization_barrier((query_weight, picked))
    own = lax.all_gather(query_weight, "zl", axis=0)
    picked = lax.all_gather(picked, "zh", axis=0)
    merge_weight, embeds, grad_resid, img_dest, picked = lax.optimization_barrier(
        (merge_weight, embeds, grad_resid, img_dest, picked)
    )
    merge_full = lax.all_gather(merge_weight, DP, axis=0)
    inputs = jnp.take(embeds, positions, axis=0, mode="clip").T
    residual = jnp.take(grad_resid, positions, axis=0, mode="clip").T
    gain = norm_gain[:, None]
    wide = inputs.astype(jnp.float32)
    squares = jnp.sum(wide * wide, axis=0)
    is_live = jnp.arange(image_count, dtype=jnp.int32) < img_count[0]
    target_dev = img_dest[0]
    dest_hot = (
        (target_dev[:, None] == jnp.arange(groups, dtype=jnp.int32)[None, :]) & is_live[:, None]
    ).astype(jnp.int32)
    earlier = jnp.cumsum(dest_hot, axis=0) - dest_hot
    slot_index = jnp.sum(earlier * dest_hot, axis=1)
    pitch = capacity * (width // LANES)
    target = jnp.where(is_live, target_dev * pitch + slot_index, -groups * pitch)

    scaled_input = gain * wide
    own, picked, inputs, residual, norm_gain, squares, scaled_input, target = (
        lax.optimization_barrier(
            (own, picked, inputs, residual, norm_gain, squares, scaled_input, target)
        )
    )
    other = lax.ppermute(own, "core", [(0, 1), (1, 0)])
    place = jnp.stack([lax.axis_index("core"), lax.axis_index("zh")]).astype(jnp.int32)
    blocks, height, depth = own.shape
    own_value, turned = in_vmem(
        own_kernel,
        [
            jax.ShapeDtypeStruct((blocks, height, side * image_count), jnp.bfloat16),
            jax.ShapeDtypeStruct((depth, side * image_count), jnp.bfloat16),
        ],
        picked,
        own,
    )
    partial_value = in_vmem(
        join_kernel,
        jax.ShapeDtypeStruct((side, blocks, 2 * height, image_count), jnp.bfloat16),
        place,
        own_value,
        turned,
        other,
        scalars=True,
    )
    partial_value = partial_value.reshape(shares, width, image_count)
    swapped = lax.all_to_all(partial_value, TP, 0, 0, tiled=True)
    normal_grad = jnp.sum(swapped.astype(jnp.float32), axis=0).astype(jnp.bfloat16)
    exchange = [
        (h * side + (a + h) % side, a * side + h) for a in range(side) for h in range(side)
    ]
    normal_grad = lax.ppermute(normal_grad, ("zh", "x"), exchange)
    stats = in_vmem(
        stat_kernel,
        jax.ShapeDtypeStruct((shares, 2, image_count), jnp.float32),
        normal_grad,
        scaled_input,
        squares[None],
    )
    stats = lax.all_to_all(stats, TP, 0, 0, tiled=True)
    outbox = in_vmem(
        functools.partial(handoff_kernel, capacity),
        jax.ShapeDtypeStruct((groups * pitch, LANES), jnp.bfloat16),
        normal_grad,
        inputs,
        residual,
        norm_gain[None],
        stats,
        target[None],
    )
    outbox, merge_pre = lax.optimization_barrier((outbox, merge_pre))
    slope = gelu_slope(merge_pre)
    received = lax.all_to_all(outbox.reshape(groups, pitch, LANES), DP, 0, 0, tiled=True)
    received, slope = lax.optimization_barrier((received, slope))
    partial_hidden = in_vmem(
        functools.partial(merge_kernel, capacity),
        jax.ShapeDtypeStruct((shares, merge_weight.shape[0], 2 * rows), jnp.bfloat16),
        received.reshape(groups * pitch, LANES),
        merge_full,
    )
    hidden = lax.all_to_all(partial_hidden, TP, 0, 0, tiled=True)
    return in_vmem(
        finish_kernel,
        jax.ShapeDtypeStruct((rows, columns), jnp.float32),
        hidden,
        slope,
    )


def solution(mesh):
    split = Mesh(mesh.devices.reshape(4, 4, 2, 4, 4), DP + TP)
    in_specs = (
        P(DP, TP),
        P(DP, TP),
        P(DP, TP),
        P(DP, TP),
        P(TP),
        P(DP, None),
        P(DP),
        P(DP, None),
        P(DP, TP),
        P(DP, TP),
    )
    out_specs = P(DP, TP)
    return jax.shard_map(local, mesh=split, in_specs=in_specs, out_specs=out_specs, check_vma=False)
```

```python
import functools

import jax
import jax.numpy as jnp
from jax import lax
from jax.experimental import pallas as pl
from jax.experimental.pallas import tpu as pltpu
from jax.sharding import Mesh
from jax.sharding import PartitionSpec as P

D = 8192
NORM_EPS = 1e-06
MIB = 1024 * 1024
LANES = 128
DP = ("zh", "zl", "core")
TP = ("x", "y")


def gelu_slope(pre):
    value = pre.astype(jnp.float32)
    cdf_part = 0.5 * (1.0 + lax.erf(value * 0.7071067811865476))
    pdf_part = jnp.exp(-0.5 * value * value) * 0.3989422804014327
    return cdf_part + value * pdf_part


def own_kernel(rows_ref, weight_ref, out_ref, turned_ref):
    parts, count, depth = rows_ref.shape
    turned_ref[...] = rows_ref[...].reshape(parts * count, depth).T
    for block in range(weight_ref.shape[0]):
        product = jnp.dot(weight_ref[block], turned_ref[...], preferred_element_type=jnp.float32)
        out_ref[block] = product.astype(out_ref.dtype)


def join_kernel(place_ref, own_ref, turned_ref, weight_ref, out_ref):
    parts, blocks, _, count = out_ref.shape
    height = weight_ref.shape[1]
    core, shift = place_ref[0], place_ref[1]
    spots = [
        pl.ds(pl.multiple_of(place * height, height), height) for place in (core, 1 - core)
    ]
    for block in range(blocks):
        product = jnp.dot(weight_ref[block], turned_ref[...], preferred_element_type=jnp.float32)
        halves = (own_ref[block], product.astype(out_ref.dtype))
        for spot, half in zip(spots, halves):
            for part in range(parts):
                out_ref[lax.rem(part + shift, parts), block, spot] = half[
                    :, part * count : (part + 1) * count
                ]


def in_vmem(kernel, out_shape, *args, scalars=False):
    specs = [pl.BlockSpec(memory_space=pltpu.VMEM) for _ in args]
    if scalars:
        specs[0] = pl.BlockSpec(memory_space=pltpu.SMEM)
    return pl.pallas_call(
        kernel,
        in_specs=specs,
        out_specs=jax.tree.map(lambda _: pl.BlockSpec(memory_space=pltpu.VMEM), out_shape),
        out_shape=out_shape,
        compiler_params=pltpu.CompilerParams(vmem_limit_bytes=24 * MIB),
    )(*args)


def finish_kernel(hidden_ref, slope_ref, out_ref):
    _, height, double = hidden_ref.shape
    rows = double // 2
    total = hidden_ref[0].astype(jnp.float32)
    for share in range(1, hidden_ref.shape[0]):
        total += hidden_ref[share].astype(jnp.float32)
    for half in range(2):
        piece = total[:, half * rows : (half + 1) * rows].T
        spot = slice(half * height, (half + 1) * height)
        out_ref[:, spot] = piece * slope_ref[:, spot]


def stat_kernel(grad_ref, scaled_ref, square_ref, out_ref):
    inner = jnp.sum(
        grad_ref[...].astype(jnp.float32) * scaled_ref[...], axis=0, keepdims=True
    )
    stats = jnp.concatenate([square_ref[...], inner], axis=0)
    for share in range(out_ref.shape[0]):
        out_ref[share] = stats


def handoff_kernel(capacity, grad_ref, input_ref, resid_ref, gain_ref, stat_ref, target_ref, *out_refs):
    width, count = grad_ref.shape
    stats = jnp.sum(stat_ref[...], axis=0)
    inverse = lax.rsqrt(stats[0:1] / D + NORM_EPS)
    factor = inverse * inverse * inverse * stats[1:2] / D
    equal = lax.broadcasted_iota(jnp.int32, (LANES, LANES), 0) == lax.broadcasted_iota(
        jnp.int32, (LANES, LANES), 1
    )
    gain = jnp.concatenate(
        [
            jnp.sum(
                jnp.where(equal, gain_ref[:, at : at + LANES], 0.0), axis=1, keepdims=True
            )
            for at in range(0, width, LANES)
        ],
        axis=0,
    )
    scaled = gain * grad_ref[...].astype(jnp.float32)
    handoff = (
        resid_ref[...].astype(jnp.float32)
        + inverse * scaled
        - input_ref[...].astype(jnp.float32) * factor
    ).astype(jnp.bfloat16)
    for number, out_ref in enumerate(out_refs):
        place = lax.broadcasted_iota(jnp.int32, (out_ref.shape[0], count), 0)
        place = place - target_ref[number : number + 1]
        total = jnp.zeros(out_ref.shape, jnp.float32)
        for block in range(width // LANES):
            hot = (place == block * capacity).astype(jnp.bfloat16)
            total += lax.dot_general(
                hot,
                handoff[block * LANES : (block + 1) * LANES],
                (((1,), (1,)), ((), ())),
                preferred_element_type=jnp.float32,
            )
        out_ref[...] = total.astype(out_ref.dtype)


def merge_kernel(capacity, place_ref, box_ref, weight_ref, out_ref):
    width = weight_ref.shape[2]
    rows = out_ref.shape[2] // 2
    chunks = width // LANES
    box = box_ref[...]
    row = lax.broadcasted_iota(jnp.int32, (rows, box.shape[0]), 0)
    spot = lax.broadcasted_iota(jnp.int32, (rows, box.shape[0]), 1)
    source = (row * 10923) >> 16
    pitch = capacity * chunks
    crossed = (source & 1) ^ place_ref[0]
    ahead = spot - (((source >> 1) * 2 + crossed) * pitch + row - source * capacity)
    pieces = []
    for block in range(chunks):
        hot = (ahead == block * capacity).astype(jnp.bfloat16)
        piece = jnp.dot(hot, box, preferred_element_type=jnp.float32)
        pieces.append(piece.T.astype(jnp.bfloat16))
    turned = jnp.concatenate(pieces, axis=0)
    for share in range(out_ref.shape[0]):
        for half in range(2):
            product = jnp.dot(
                weight_ref[2 * share + half], turned, preferred_element_type=jnp.float32
            )
            out_ref[share, :, half * rows : (half + 1) * rows] = product.astype(out_ref.dtype)


def local(
    grad_query,
    query_weight,
    grad_resid,
    embeds,
    norm_gain,
    img_pos,
    img_count,
    img_dest,
    merge_weight,
    merge_pre,
):
    groups = lax.axis_size(DP)
    shares = lax.axis_size(TP)
    side = lax.axis_size("zh")
    rows, columns = merge_pre.shape
    capacity = rows // groups
    positions = img_pos[0]
    image_count = positions.shape[0]
    width = embeds.shape[1]

    picked = jnp.take(grad_query, positions, axis=0, mode="clip")
    query_weight, picked = lax.optimization_barrier((query_weight, picked))
    own = lax.all_gather(query_weight, "zl", axis=0)
    picked = lax.all_gather(picked, "zh", axis=0)
    merge_weight, embeds, grad_resid, img_dest, picked = lax.optimization_barrier(
        (merge_weight, embeds, grad_resid, img_dest, picked)
    )
    merge_full = lax.all_gather(merge_weight, DP, axis=0)
    inputs = jnp.take(embeds, positions, axis=0, mode="clip").T
    residual = jnp.take(grad_resid, positions, axis=0, mode="clip").T
    gain = norm_gain[:, None]
    wide = inputs.astype(jnp.float32)
    squares = jnp.sum(wide * wide, axis=0)
    is_live = jnp.arange(image_count, dtype=jnp.int32) < img_count[0]
    target_dev = img_dest[0]
    dest_hot = (
        (target_dev[:, None] == jnp.arange(groups, dtype=jnp.int32)[None, :]) & is_live[:, None]
    ).astype(jnp.int32)
    earlier = jnp.cumsum(dest_hot, axis=0) - dest_hot
    slot_index = jnp.sum(earlier * dest_hot, axis=1)
    pitch = capacity * (width // LANES)
    planes = groups // 2
    crosses = target_dev % 2 != lax.axis_index("core")
    target = (target_dev // 2) * pitch + slot_index
    target = jnp.stack(
        [
            jnp.where(is_live & ~crosses, target, -planes * pitch),
            jnp.where(is_live & crosses, target, -planes * pitch),
        ]
    )

    scaled_input = gain * wide
    own, picked, inputs, residual, norm_gain, squares, scaled_input, target = (
        lax.optimization_barrier(
            (own, picked, inputs, residual, norm_gain, squares, scaled_input, target)
        )
    )
    other = lax.ppermute(own, "core", [(0, 1), (1, 0)])
    place = jnp.stack([lax.axis_index("core"), lax.axis_index("zh")]).astype(jnp.int32)
    blocks, height, depth = own.shape
    own_value, turned = in_vmem(
        own_kernel,
        [
            jax.ShapeDtypeStruct((blocks, height, side * image_count), jnp.bfloat16),
            jax.ShapeDtypeStruct((depth, side * image_count), jnp.bfloat16),
        ],
        picked,
        own,
    )
    partial_value = in_vmem(
        join_kernel,
        jax.ShapeDtypeStruct((side, blocks, 2 * height, image_count), jnp.bfloat16),
        place,
        own_value,
        turned,
        other,
        scalars=True,
    )
    partial_value = partial_value.reshape(shares, width, image_count)
    swapped = lax.all_to_all(partial_value, TP, 0, 0, tiled=True)
    normal_grad = jnp.sum(swapped.astype(jnp.float32), axis=0).astype(jnp.bfloat16)
    exchange = [
        (h * side + (a + h) % side, a * side + h) for a in range(side) for h in range(side)
    ]
    normal_grad = lax.ppermute(normal_grad, ("zh", "x"), exchange)
    stats = in_vmem(
        stat_kernel,
        jax.ShapeDtypeStruct((shares, 2, image_count), jnp.float32),
        normal_grad,
        scaled_input,
        squares[None],
    )
    stats = lax.all_to_all(stats, TP, 0, 0, tiled=True)
    outbox, across = in_vmem(
        functools.partial(handoff_kernel, capacity),
        [jax.ShapeDtypeStruct((planes * pitch, LANES), jnp.bfloat16)] * 2,
        normal_grad,
        inputs,
        residual,
        norm_gain[None],
        stats,
        target,
    )
    outbox, merge_pre = lax.optimization_barrier((outbox, merge_pre))
    slope = gelu_slope(merge_pre)
    across = lax.ppermute(across, "core", [(0, 1), (1, 0)])
    outbox = jnp.concatenate(
        [box.reshape(planes, pitch, LANES) for box in (outbox, across)], axis=1
    )
    received = lax.all_to_all(outbox, ("zh", "zl"), 0, 0, tiled=True)
    received, slope = lax.optimization_barrier((received, slope))
    partial_hidden = in_vmem(
        functools.partial(merge_kernel, capacity),
        jax.ShapeDtypeStruct((shares, merge_weight.shape[0], 2 * rows), jnp.bfloat16),
        place,
        received.reshape(groups * pitch, LANES),
        merge_full,
        scalars=True,
    )
    hidden = lax.all_to_all(partial_hidden, TP, 0, 0, tiled=True)
    return in_vmem(
        finish_kernel,
        jax.ShapeDtypeStruct((rows, columns), jnp.float32),
        hidden,
        slope,
    )


def solution(mesh):
    split = Mesh(mesh.devices.reshape(4, 4, 2, 4, 4), DP + TP)
    in_specs = (
        P(DP, TP),
        P(DP, TP),
        P(DP, TP),
        P(DP, TP),
        P(TP),
        P(DP, None),
        P(DP),
        P(DP, None),
        P(DP, TP),
        P(DP, TP),
    )
    out_specs = P(DP, TP)
    return jax.shard_map(local, mesh=split, in_specs=in_specs, out_specs=out_specs, check_vma=False)
```

```python
import jax
import jax.numpy as jnp
from jax import lax
from jax.experimental import pallas as pl
from jax.experimental.pallas import tpu as pltpu
from jax.sharding import Mesh
from jax.sharding import PartitionSpec as P

D = 8192
NORM_EPS = 1e-06
MIB = 1024 * 1024
LANES = 128
SLOT_PITCH = 8
DP = ("zh", "zl", "core")
TP = ("x", "y")


def gelu_slope(pre):
    value = pre.astype(jnp.float32)
    cdf_part = 0.5 * (1.0 + lax.erf(value * 0.7071067811865476))
    pdf_part = jnp.exp(-0.5 * value * value) * 0.3989422804014327
    return cdf_part + value * pdf_part


def own_kernel(rows_ref, weight_ref, out_ref, turned_ref):
    parts, count, depth = rows_ref.shape
    turned_ref[...] = rows_ref[...].reshape(parts * count, depth).T
    for block in range(weight_ref.shape[0]):
        product = jnp.dot(weight_ref[block], turned_ref[...], preferred_element_type=jnp.float32)
        out_ref[block] = product.astype(out_ref.dtype)


def join_kernel(place_ref, own_ref, turned_ref, weight_ref, out_ref):
    parts, blocks, _, count = out_ref.shape
    height = weight_ref.shape[1]
    core, shift = place_ref[0], place_ref[1]
    spots = [
        pl.ds(pl.multiple_of(place * height, height), height) for place in (core, 1 - core)
    ]
    for block in range(blocks):
        product = jnp.dot(weight_ref[block], turned_ref[...], preferred_element_type=jnp.float32)
        halves = (own_ref[block], product.astype(out_ref.dtype))
        for spot, half in zip(spots, halves):
            for part in range(parts):
                out_ref[lax.rem(part + shift, parts), block, spot] = half[
                    :, part * count : (part + 1) * count
                ]


def in_vmem(kernel, out_shape, *args, scalars=False):
    specs = [pl.BlockSpec(memory_space=pltpu.VMEM) for _ in args]
    if scalars:
        specs[0] = pl.BlockSpec(memory_space=pltpu.SMEM)
    return pl.pallas_call(
        kernel,
        in_specs=specs,
        out_specs=jax.tree.map(lambda _: pl.BlockSpec(memory_space=pltpu.VMEM), out_shape),
        out_shape=out_shape,
        compiler_params=pltpu.CompilerParams(vmem_limit_bytes=24 * MIB),
    )(*args)


def send_kernel(hidden_ref, target_ref, out_ref):
    count = target_ref.shape[1]
    total = jnp.sum(hidden_ref[...].astype(jnp.float32), axis=0).astype(jnp.bfloat16)
    spare = out_ref.shape[1] - 2 * total.shape[0]
    columns = jnp.concatenate(
        [total[:, :count], total[:, count:], jnp.zeros((spare, count), jnp.bfloat16)], axis=0
    )
    row = lax.broadcasted_iota(jnp.int32, (out_ref.shape[0], count), 0)
    hot = (row == target_ref[...]).astype(jnp.bfloat16)
    out_ref[...] = lax.dot_general(
        hot, columns, (((1,), (1,)), ((), ())), preferred_element_type=jnp.float32
    ).astype(out_ref.dtype)


def finish_kernel(box_ref, spot_ref, slope_ref, out_ref):
    rows, columns = out_ref.shape
    spot = lax.broadcasted_iota(jnp.int32, (rows, box_ref.shape[0]), 1)
    hot = (spot == spot_ref[...]).astype(jnp.bfloat16)
    hidden = jnp.dot(hot, box_ref[...], preferred_element_type=jnp.float32)
    out_ref[...] = hidden[:, :columns] * slope_ref[...]


def stat_kernel(grad_ref, scaled_ref, square_ref, out_ref):
    inner = jnp.sum(
        grad_ref[...].astype(jnp.float32) * scaled_ref[...], axis=0, keepdims=True
    )
    stats = jnp.concatenate([square_ref[...], inner], axis=0)
    for share in range(out_ref.shape[0]):
        out_ref[share] = stats


def merge_kernel(grad_ref, input_ref, resid_ref, gain_ref, stat_ref, weight_ref, out_ref):
    width, count = grad_ref.shape
    stats = jnp.sum(stat_ref[...], axis=0)
    inverse = lax.rsqrt(stats[0:1] / D + NORM_EPS)
    factor = inverse * inverse * inverse * stats[1:2] / D
    equal = lax.broadcasted_iota(jnp.int32, (LANES, LANES), 0) == lax.broadcasted_iota(
        jnp.int32, (LANES, LANES), 1
    )
    gain = jnp.concatenate(
        [
            jnp.sum(
                jnp.where(equal, gain_ref[:, at : at + LANES], 0.0), axis=1, keepdims=True
            )
            for at in range(0, width, LANES)
        ],
        axis=0,
    )
    scaled = gain * grad_ref[...].astype(jnp.float32)
    handoff = (
        resid_ref[...].astype(jnp.float32)
        + inverse * scaled
        - input_ref[...].astype(jnp.float32) * factor
    ).astype(jnp.bfloat16)
    for share in range(out_ref.shape[0]):
        for half in range(2):
            product = jnp.dot(
                weight_ref[2 * share + half], handoff, preferred_element_type=jnp.float32
            )
            out_ref[share, :, half * count : (half + 1) * count] = product.astype(out_ref.dtype)


def local(
    grad_query,
    query_weight,
    grad_resid,
    embeds,
    norm_gain,
    img_pos,
    img_count,
    img_dest,
    merge_weight,
    merge_pre,
):
    groups = lax.axis_size(DP)
    shares = lax.axis_size(TP)
    side = lax.axis_size("zh")
    rows, columns = merge_pre.shape
    capacity = rows // groups
    positions = img_pos[0]
    image_count = positions.shape[0]
    width = embeds.shape[1]

    picked = jnp.take(grad_query, positions, axis=0, mode="clip")
    query_weight, picked = lax.optimization_barrier((query_weight, picked))
    own = lax.all_gather(query_weight, "zl", axis=0)
    picked = lax.all_gather(picked, "zh", axis=0)
    merge_weight, embeds, grad_resid, img_dest, picked = lax.optimization_barrier(
        (merge_weight, embeds, grad_resid, img_dest, picked)
    )
    merge_full = lax.all_gather(merge_weight, DP, axis=0)
    inputs = jnp.take(embeds, positions, axis=0, mode="clip").T
    residual = jnp.take(grad_resid, positions, axis=0, mode="clip").T
    gain = norm_gain[:, None]
    wide = inputs.astype(jnp.float32)
    squares = jnp.sum(wide * wide, axis=0)
    is_live = jnp.arange(image_count, dtype=jnp.int32) < img_count[0]
    target_dev = img_dest[0]
    dest_hot = (
        (target_dev[:, None] == jnp.arange(groups, dtype=jnp.int32)[None, :]) & is_live[:, None]
    ).astype(jnp.int32)
    earlier = jnp.cumsum(dest_hot, axis=0) - dest_hot
    slot_index = jnp.sum(earlier * dest_hot, axis=1)
    target = jnp.where(is_live, target_dev * SLOT_PITCH + slot_index, -1)
    number = jnp.arange(rows, dtype=jnp.int32)
    spot = number // capacity * SLOT_PITCH + number % capacity
    scaled_input = gain * wide
    own, picked, inputs, residual, norm_gain, squares, scaled_input, target, spot = (
        lax.optimization_barrier(
            (own, picked, inputs, residual, norm_gain, squares, scaled_input, target, spot)
        )
    )
    other = lax.ppermute(own, "core", [(0, 1), (1, 0)])
    place = jnp.stack([lax.axis_index("core"), lax.axis_index("zh")]).astype(jnp.int32)
    blocks, height, depth = own.shape
    own_value, turned = in_vmem(
        own_kernel,
        [
            jax.ShapeDtypeStruct((blocks, height, side * image_count), jnp.bfloat16),
            jax.ShapeDtypeStruct((depth, side * image_count), jnp.bfloat16),
        ],
        picked,
        own,
    )
    partial_value = in_vmem(
        join_kernel,
        jax.ShapeDtypeStruct((side, blocks, 2 * height, image_count), jnp.bfloat16),
        place,
        own_value,
        turned,
        other,
        scalars=True,
    )
    partial_value = partial_value.reshape(shares, width, image_count)
    swapped = lax.all_to_all(partial_value, TP, 0, 0, tiled=True)
    normal_grad = jnp.sum(swapped.astype(jnp.float32), axis=0).astype(jnp.bfloat16)
    exchange = [
        (h * side + (a + h) % side, a * side + h) for a in range(side) for h in range(side)
    ]
    normal_grad = lax.ppermute(normal_grad, ("zh", "x"), exchange)
    stats = in_vmem(
        stat_kernel,
        jax.ShapeDtypeStruct((shares, 2, image_count), jnp.float32),
        normal_grad,
        scaled_input,
        squares[None],
    )
    stats = lax.all_to_all(stats, TP, 0, 0, tiled=True)
    partial_hidden = in_vmem(
        merge_kernel,
        jax.ShapeDtypeStruct((shares, merge_weight.shape[0], 2 * image_count), jnp.bfloat16),
        normal_grad,
        inputs,
        residual,
        norm_gain[None],
        stats,
        merge_full,
    )
    hidden = lax.all_to_all(partial_hidden, TP, 0, 0, tiled=True)
    lanes = -(-columns // LANES) * LANES
    outbox = in_vmem(
        send_kernel,
        jax.ShapeDtypeStruct((groups * SLOT_PITCH, lanes), jnp.bfloat16),
        hidden,
        target[None],
    )
    outbox, merge_pre = lax.optimization_barrier((outbox, merge_pre))
    slope = gelu_slope(merge_pre)
    received = lax.all_to_all(outbox.reshape(groups, SLOT_PITCH, lanes), DP, 0, 0, tiled=True)
    return in_vmem(
        finish_kernel,
        jax.ShapeDtypeStruct((rows, columns), jnp.float32),
        received.reshape(groups * SLOT_PITCH, lanes),
        spot[:, None],
        slope,
    )


def solution(mesh):
    split = Mesh(mesh.devices.reshape(4, 4, 2, 4, 4), DP + TP)
    in_specs = (
        P(DP, TP),
        P(DP, TP),
        P(DP, TP),
        P(DP, TP),
        P(TP),
        P(DP, None),
        P(DP),
        P(DP, None),
        P(DP, TP),
        P(DP, TP),
    )
    out_specs = P(DP, TP)
    return jax.shard_map(local, mesh=split, in_specs=in_specs, out_specs=out_specs, check_vma=False)
```
